256 devices in a mesh: ctx: 16 (over x, y_hi, core), exp: 16 (over y_lo, z).
Axes of the slice: x: 4, y: 4 (y_hi: 2, y_lo: 2; y = y_hi * 2 + y_lo), z: 8, core: 2. Of those that a mesh axis runs over, the one named last changes fastest.
Arguments:
- query: bfloat16 [16, 2048, 12288], P('exp', 'ctx'), may hold values from -8 to 8
- out_grad: bfloat16 [16, 2048, 8192], P('exp', 'ctx'), may hold values from -6 to 6
- latent: bfloat16 [16, 2048, 512], P('exp', 'ctx'), may hold values from -6 to 6
- rope_key: bfloat16 [16, 2048, 64], P('exp', 'ctx'), may hold values from -8 to 8
- w_key: bfloat16 [512, 8192], P(None, 'ctx'), may hold values from -0.25 to 0.25
- w_value: bfloat16 [512, 8192], P(None, 'ctx'), may hold values from -0.25 to 0.25
- grad_stream: bfloat16 [16, 2048, 5120], P('exp', 'ctx'), may hold values from -6 to 6
- expert_ids: int32 [16, 2048, 6], P('exp', 'ctx'), may hold values from 0 to 159, all different within a row; in each aligned block of 128 rows (0 to 127, 128 to 255, ..., all dimensions but the last counted through in order) at most 6 rows name the same one
- gate_weights: bfloat16 [16, 2048, 6], P('exp', 'ctx'), may hold values from 0.049804688 to 0.5
- saved_hidden: bfloat16 [16, 16, 96, 1536], P('ctx', 'exp'), may hold values from -6 to 6
- w_down: bfloat16 [16, 1536, 5120], P('exp', None, 'ctx'), may hold values from -0.15625 to 0.15625
Outputs:
- query_grad: bfloat16 [16, 2048, 12288], P('exp', 'ctx')
- latent_grad: bfloat16 [16, 2048, 512], P('exp', 'ctx')
- rope_grad: bfloat16 [16, 2048, 64], P('exp', 'ctx')
- hidden_grad: bfloat16 [16, 16, 96, 1536], P('ctx', 'exp')
- gate_grad: float32 [16, 2048, 6], P('exp', 'ctx')
The draws below stay inside these ranges and needn't reach their ends.
Inputs may be any that keep to these rules, and one draw needn't show every extreme that they name: `expert_ids`: each token names 6 distinct experts; within the 128 tokens of one device no expert is named by more than 6 tokens, a bound that some block reaches.
All inputs are finite; a program needn't handle non-finite values.
Results may differ from the reference program's by a relative error of at most 0.015.
Values may be sent and summed in bfloat16 or wider, within the bound.
No kernel may reach another device: no remote copies, remote signals or barrier semaphores. Data moves between devices by JAX's collectives and lax.ppermute only.
A program may use at most 192 MiB of HBM per device.

```python
import math
import jax
import jax.numpy as jnp
import numpy as np
from jax import lax

D = 5120
HEADS = 64
NOPE = 128
ROPE = 64
VDIM = 128
LATENT = 512
FFH = 1536
EXPERTS = 160
TOPK = 6
TOK_DEV = 128
WIN = 32
CAP = 6
SEQ = 2048
STREAMS = 16
N_CTX = 16
N_EXP = 16


def draw_rope_key(key, part):
    key = jax.random.fold_in(key, 5)
    drawn = jax.random.normal(key, (STREAMS, SEQ, ROPE), jnp.float32)
    return jnp.clip(drawn, -6.0, 6.0).astype(jnp.bfloat16)


def draw_query(key, part):
    key = jax.random.fold_in(key, 6)
    drawn = jax.random.normal(key, (STREAMS, SEQ, HEADS * (NOPE + ROPE)), jnp.float32)
    return jnp.clip(drawn, -6.0, 6.0).astype(jnp.bfloat16)


def level_of(stream_key, dims, shards, low, largest):
    def one(axis_at, parts):
        steps = jax.random.uniform(jax.random.fold_in(jax.random.fold_in(stream_key, 6), axis_at), (parts,), jnp.float32, low / len(shards), largest / len(shards))
        return jnp.repeat(jnp.exp(steps), dims[axis_at] // parts).reshape((-1,) + (1,) * (len(dims) - axis_at - 1))

    gain = one(*shards[0])
    for cut in shards[1:]:
        gain = gain * one(*cut)
    return gain


def deal_out(key, own, number, rows, number_of, top, most, lean):
    order = jax.random.permutation(key, number_of)
    heavy_load, common = portions_of(number_of, rows * top, most, lean, True), portions_of(number_of, rows * top, most, lean, False)
    places = jnp.arange(number_of)

    def named(tallies, turn):
        used = int((tallies > 0).sum())
        fixed = max(1, used // 4)
        moved = fixed + (places - fixed + turn * (used - fixed)) % max(1, number_of - fixed)
        return jnp.zeros((number_of,), jnp.int32).at[order[jnp.where(places < fixed, places, moved)]].set(jnp.asarray(tallies, jnp.int32))

    tallies = jnp.where(number % 4 == 0, named(heavy_load, number // 4), named(common, number - number // 4 - 1))
    mixed = jax.random.permutation(jax.random.fold_in(own, 3), number_of)
    giver, sink = mixed[0:number_of // 2 * 2:2], mixed[1:number_of // 2 * 2:2]
    margin = jnp.minimum(tallies[giver] - 1, most - tallies[sink]) // 2
    margin = jnp.where((giver == order[0]) | (sink == order[0]) | (tallies[sink] == 0), 0, jnp.maximum(margin, 0))
    moved = jax.random.randint(jax.random.fold_in(own, 4), (number_of // 2,), 0, 1 << 20) % (margin + 1)
    tallies = tallies.at[giver].add(-moved).at[sink].add(moved)
    members = jnp.searchsorted(jnp.cumsum(tallies), jnp.arange(rows * top), side="right").astype(jnp.int32)
    listing = members.reshape(top, rows).T
    listing = listing[jax.random.permutation(jax.random.fold_in(own, 1), rows)]
    turn = jax.random.randint(jax.random.fold_in(own, 2), (rows, 1), 0, top)
    return jnp.take_along_axis(listing, (jnp.arange(top)[None, :] + turn) % top, axis=1)


def portions_of(count, total, limit, skew, full):
    loads = [(1 << 20) // math.isqrt(grade ** skew) + 1 for grade in range(1, count + 1)]
    largest = limit if full else min(limit, max(-(-total // count), total * loads[0] // sum(loads)))
    least = 1 if total - largest >= count - 1 else 0
    counts, rest = [largest] + [least] * (count - 1), total - largest - least * (count - 1)
    while rest > 0:
        free = [i for i in range(1, count) if counts[i] < largest] or [i for i in range(1, count) if counts[i] < limit]
        whole, left = sum([loads[i] for i in free]), rest
        for i in free:
            addition = min(limit - counts[i], max(1, left * loads[i] // whole), rest)
            counts[i] = counts[i] + addition
            rest = rest - addition
    return np.array(counts)


def gaussian(own_key, shape, width, bound, pieces=(), held_as=jnp.bfloat16):
    entries = width * jax.random.normal(own_key, shape, jnp.float32)
    if pieces:
        entries = entries * level_of(own_key, shape, pieces, -0.22, 0.18)
    return jnp.clip(entries, -bound, bound).astype(held_as)


def setup_inputs(seed: int = 0) -> dict:
    streams_of = jax.random.split(jax.random.key(seed), 12)
    query = draw_query(jax.random.fold_in(streams_of[11], 71), 0)
    out_grad = gaussian(streams_of[1], (STREAMS, SEQ, HEADS * VDIM), 1.0, 6.0, ((0, 16), (1, 16)))
    latent = gaussian(streams_of[2], (STREAMS, SEQ, LATENT), 1.0, 6.0, ((0, 16), (1, 16)))
    rope_key = draw_rope_key(jax.random.fold_in(streams_of[11], 71), 0)
    w_key = gaussian(streams_of[4], (LATENT, HEADS * NOPE), LATENT ** -0.5, 0.25, ((1, 16),))
    w_value = gaussian(streams_of[5], (LATENT, HEADS * VDIM), LATENT ** -0.5, 0.25, ((1, 16),))
    grad_stream = gaussian(streams_of[6], (STREAMS, SEQ, D), 1.0, 6.0, ((0, 16), (1, 16)))
    expert_ids_keys = jax.random.split(jax.random.fold_in(streams_of[7], 1), STREAMS * SEQ // TOK_DEV)
    expert_ids_turns = jax.random.permutation(jax.random.fold_in(streams_of[7], 3), STREAMS * SEQ // TOK_DEV)
    expert_ids = jax.vmap(lambda own, number: deal_out(jax.random.fold_in(streams_of[7], 2), own, number, TOK_DEV, EXPERTS, TOPK, CAP, 2))(expert_ids_keys, expert_ids_turns).reshape((STREAMS, SEQ, TOPK))
    gate_weights = jnp.clip(0.049804688 + 0.4501953 * jax.random.uniform(streams_of[8], (STREAMS, SEQ, TOPK), jnp.float32) ** level_of(streams_of[8], (STREAMS, SEQ, TOPK), ((0, 16), (1, 16)), -0.2, 0.2), 0.049804688, 0.5).astype(jnp.bfloat16)
    saved_hidden = gaussian(streams_of[9], (N_CTX, N_EXP, N_EXP * CAP, FFH), 1.0, 6.0, ((0, 16), (1, 16)))
    w_down = gaussian(streams_of[10], (N_EXP, FFH, D), FFH ** -0.5, 0.15625, ((0, 16), (2, 16)))
    return dict(query=query, out_grad=out_grad, latent=latent, rope_key=rope_key, w_key=w_key, w_value=w_value, grad_stream=grad_stream, expert_ids=expert_ids, gate_weights=gate_weights, saved_hidden=saved_hidden, w_down=w_down)


def route_plan(expert_ids, owners, capacity):
    share = EXPERTS // owners
    flat_ids = expert_ids.reshape(-1)
    active = flat_ids % share == 0
    owner_of = jnp.where(active, flat_ids // share, -1)
    owner_hot = (owner_of[:, None] == jnp.arange(owners, dtype=jnp.int32)[None, :]).astype(jnp.int32)
    earlier = jnp.cumsum(owner_hot, axis=0) - owner_hot
    slot_of = jnp.sum(earlier * owner_hot, axis=1)
    target = jnp.where(active, owner_of * capacity + slot_of, -1)
    slot_ids = jnp.arange(owners * capacity, dtype=jnp.int32)
    return (target[:, None] == slot_ids[None, :]).astype(jnp.float32)


def window_mask(block_index, rows):
    query_rel = jnp.arange(rows, dtype=jnp.int32)[:, None]
    key_rel = jnp.arange(2 * rows, dtype=jnp.int32)[None, :]
    inside = (key_rel > query_rel) & (key_rel <= query_rel + rows)
    return inside & ((block_index > 0) | (key_rel >= rows))


def attend_stream(inputs, w_key, w_value):
    query, out_grad, latent, rope_key = inputs
    seq_len = query.shape[0]
    blocks = seq_len // WIN
    score_scale = (NOPE + ROPE) ** -0.5
    q_all = query.reshape(seq_len, HEADS, NOPE + ROPE).astype(jnp.float32)
    d_all = out_grad.reshape(seq_len, HEADS, VDIM).astype(jnp.float32)
    key_rows = jnp.dot(latent, w_key, preferred_element_type=jnp.float32).astype(jnp.bfloat16).astype(jnp.float32)
    value_rows = jnp.dot(latent, w_value, preferred_element_type=jnp.float32).astype(jnp.bfloat16).astype(jnp.float32)
    key_pad = jnp.concatenate([jnp.zeros((WIN, HEADS * NOPE), jnp.float32), key_rows], axis=0)
    value_pad = jnp.concatenate([jnp.zeros((WIN, HEADS * VDIM), jnp.float32), value_rows], axis=0)
    rope_pad = jnp.concatenate([jnp.zeros((WIN, ROPE), jnp.float32), rope_key.astype(jnp.float32)], axis=0)
    key_weight = w_key.astype(jnp.float32)
    value_weight = w_value.astype(jnp.float32)

    def per_block(block_index):
        start = (block_index * WIN).astype(jnp.int32)
        q_block = lax.dynamic_slice_in_dim(q_all, start, WIN, 0)
        d_block = lax.dynamic_slice_in_dim(d_all, start, WIN, 0)
        q_nope = q_block[..., :NOPE]
        q_rope = q_block[..., NOPE:]
        keys = lax.dynamic_slice_in_dim(key_pad, start, 2 * WIN, 0).reshape(2 * WIN, HEADS, NOPE)
        values = lax.dynamic_slice_in_dim(value_pad, start, 2 * WIN, 0).reshape(2 * WIN, HEADS, VDIM)
        ropes = lax.dynamic_slice_in_dim(rope_pad, start, 2 * WIN, 0)
        allowed = window_mask(block_index, WIN)
        raw_scores = jnp.einsum('ihd,jhd->hij', q_nope, keys) + jnp.einsum('ihd,jd->hij', q_rope, ropes)
        scores = jnp.where(allowed[None], score_scale * raw_scores, -jnp.inf)
        row_max = jnp.max(scores, axis=2, keepdims=True)
        shifted = jnp.exp(scores - row_max)
        probs = shifted / jnp.sum(shifted, axis=2, keepdims=True)
        prob_grad = jnp.einsum('ihd,jhd->hij', d_block, values)
        delta = jnp.sum(probs * prob_grad, axis=2, keepdims=True)
        score_grad = (score_scale * probs * (prob_grad - delta)).astype(jnp.bfloat16).astype(jnp.float32)
        probs_low = probs.astype(jnp.bfloat16).astype(jnp.float32)
        grad_nope = jnp.einsum('hij,jhd->ihd', score_grad, keys)
        grad_rope = jnp.einsum('hij,jd->ihd', score_grad, ropes)
        query_part = jnp.concatenate([grad_nope, grad_rope], axis=2).reshape(WIN, -1).astype(jnp.bfloat16)
        key_part = jnp.einsum('hij,ihd->jhd', score_grad, q_nope).astype(jnp.bfloat16).astype(jnp.float32)
        value_part = jnp.einsum('hij,ihd->jhd', probs_low, d_block).astype(jnp.bfloat16).astype(jnp.float32)
        latent_part = jnp.dot(key_part.reshape(2 * WIN, -1), key_weight.T, precision=lax.Precision.HIGHEST)
        latent_part = latent_part + jnp.dot(value_part.reshape(2 * WIN, -1), value_weight.T, precision=lax.Precision.HIGHEST)
        rope_part = jnp.einsum('hij,ihd->jd', score_grad, q_rope)
        return query_part, latent_part, rope_part

    query_parts, latent_parts, rope_parts = lax.map(per_block, jnp.arange(blocks, dtype=jnp.int32))
    query_grad = query_parts.reshape(seq_len, -1)
    latent_total = latent_parts[:, WIN:] + jnp.concatenate([latent_parts[1:, :WIN], jnp.zeros((1, WIN, LATENT), jnp.float32)], axis=0)
    rope_total = rope_parts[:, WIN:] + jnp.concatenate([rope_parts[1:, :WIN], jnp.zeros((1, WIN, ROPE), jnp.float32)], axis=0)
    return query_grad, latent_total.reshape(seq_len, LATENT).astype(jnp.bfloat16), rope_total.reshape(seq_len, ROPE).astype(jnp.bfloat16)


def expert_branch(grad_stream, expert_ids, gate_weights, saved_hidden, w_down):
    owners = N_EXP
    down_full = w_down.astype(jnp.float32)

    def per_block(block_index):
        start = block_index * TOK_DEV
        stream_grad = lax.dynamic_slice_in_dim(grad_stream, start, TOK_DEV, 1).astype(jnp.float32)
        block_ids = lax.dynamic_slice_in_dim(expert_ids, start, TOK_DEV, 1)
        block_gates = lax.dynamic_slice_in_dim(gate_weights, start, TOK_DEV, 1).astype(jnp.float32)
        slot_hot = jax.vmap(lambda ids: route_plan(ids, owners, CAP))(block_ids)
        token_hot = slot_hot.reshape(owners, TOK_DEV, TOPK, -1).sum(axis=2)
        outbound = jnp.einsum('sto,std->sod', token_hot, stream_grad).astype(jnp.bfloat16)
        gate_send = jnp.einsum('sao,sa->so', slot_hot, block_gates.reshape(owners, -1)).astype(jnp.bfloat16)
        routed = outbound.reshape(owners, owners, CAP, D).transpose(1, 0, 2, 3).reshape(owners, owners * CAP, D)
        row_gate = gate_send.reshape(owners, owners, CAP).transpose(1, 0, 2).reshape(owners, -1)
        raw_grad = jnp.einsum('ord,ofd->orf', routed.astype(jnp.float32), down_full)
        hidden_rows = lax.dynamic_index_in_dim(saved_hidden, block_index, 0, keepdims=False).astype(jnp.float32)
        gate_part = jnp.sum(hidden_rows * raw_grad, axis=2)
        hidden_grad = (row_gate.astype(jnp.float32)[..., None] * raw_grad).astype(jnp.bfloat16)
        returned = gate_part.reshape(owners, owners, CAP).transpose(1, 0, 2).reshape(owners, -1)
        gate_grad = jnp.sum(slot_hot * returned[:, None, :], axis=2).reshape(owners, TOK_DEV, TOPK)
        return hidden_grad, gate_grad

    hidden_grad, gate_grad = lax.map(per_block, jnp.arange(N_CTX, dtype=jnp.int32))
    gate_grad = gate_grad.transpose(1, 0, 2, 3).reshape(owners, N_CTX * TOK_DEV, TOPK)
    return hidden_grad, gate_grad


def reference(query, out_grad, latent, rope_key, w_key, w_value, grad_stream, expert_ids, gate_weights, saved_hidden, w_down):
    query_grad, latent_grad, rope_grad = lax.map(lambda pack: attend_stream(pack, w_key, w_value), (query, out_grad, latent, rope_key))
    hidden_grad, gate_grad = expert_branch(grad_stream, expert_ids, gate_weights, saved_hidden, w_down)
    return (query_grad, latent_grad, rope_grad, hidden_grad, gate_grad)
```

```python
import functools

import jax
import jax.numpy as jnp
from jax import lax
from jax.experimental import pallas as pl
from jax.experimental.pallas import tpu as pltpu
from jax.sharding import PartitionSpec as P

HEADS = 64
NOPE = 128
ROPE = 64
VDIM = 128
LATENT = 512
FFH = 1536
EXPERTS = 160
TOPK = 6
WIN = 32
CAP = 6
CTX = 16
EXP = 16
TOK = 128
CHIPS = 8
GROUP = 4
QW = GROUP * (NOPE + ROPE)
VW = GROUP * VDIM
ROWS = 2 * TOK + WIN
SPAN = TOK + WIN
SCALE = (NOPE + ROPE) ** (-0.5)
COST = pl.CostEstimate(flops=1_000_000, bytes_accessed=1_000_000, transcendentals=0)


def ctx_at(x, half, core):
    return ((x % 4) * 2 + half) * 2 + core


def ctx_moves(step):
    return [
        (ctx_at(x, half, core), ctx_at(x + step, half, core))
        for x in range(4)
        for half in range(2)
        for core in range(2)
    ]


RIGHT = ctx_moves(1)
LEFT = ctx_moves(-1)
TWIN = [(i, i ^ 1) for i in range(CTX)]
ACROSS = [
    ((i * EXP + e), ((i ^ 2) * EXP + (e ^ 8))) for i in range(CTX) for e in range(EXP)
]
RING = [[ctx_at(x, half, core) for x in range(4) for core in range(2)] for half in range(2)]
RING_CORE = [[ctx_at(x, half, core) for x in range(4)] for half in range(2) for core in range(2)]


def nothing_body(*refs):
    pass


def tie(value, *others):
    return pl.pallas_call(
        nothing_body,
        in_specs=[pl.BlockSpec(memory_space=pl.ANY)] * (1 + len(others)),
        out_specs=pl.BlockSpec(memory_space=pl.ANY),
        out_shape=jax.ShapeDtypeStruct(value.shape, value.dtype),
        input_output_aliases={0: 0},
        cost_estimate=COST,
    )(value, *others)


def stack_body(key_ref, value_ref, out_ref):
    out_ref[:LATENT] = key_ref[...]
    out_ref[LATENT:] = value_ref[...]


def stack(w_key, w_value):
    return pl.pallas_call(
        stack_body,
        out_shape=jax.ShapeDtypeStruct((2 * LATENT, VW), jnp.bfloat16),
        compiler_params=pltpu.CompilerParams(vmem_limit_bytes=60 * 1024 * 1024),
        cost_estimate=COST,
    )(w_key, w_value)


def place_body(counts, where_ref, grid_ref, *refs):
    parts, out_ref = refs[: len(counts)], refs[len(counts)]
    held, in_sems, out_sems = refs[len(counts) + 1 :]
    core = where_ref[0]
    ways = []
    for part, count in zip(parts, counts):
        for i in range(count):
            at = len(ways)
            column = pl.multiple_of((2 * where_ref[1 + at] + 1 - core) * QW, QW)
            ways.append(
                (
                    pltpu.make_async_copy(part.at[i], held.at[at], in_sems.at[at]),
                    pltpu.make_async_copy(
                        held.at[at], out_ref.at[:, pl.ds(column, QW)], out_sems.at[at]
                    ),
                )
            )
    for arrive, _ in ways:
        arrive.start()
    for arrive, leave in ways:
        arrive.wait()
        leave.start()
    for _, leave in ways:
        leave.wait()


def place(where, query_grad, parts):
    counts = tuple(part.shape[0] for part in parts)
    return pl.pallas_call(
        functools.partial(place_body, counts),
        grid_spec=pltpu.PrefetchScalarGridSpec(
            num_scalar_prefetch=1,
            grid=(),
            in_specs=[pl.BlockSpec(memory_space=pl.ANY)] * (1 + len(parts)),
            out_specs=pl.BlockSpec(memory_space=pl.ANY),
            scratch_shapes=[
                pltpu.VMEM((sum(counts), TOK, QW), jnp.bfloat16),
                pltpu.SemaphoreType.DMA((sum(counts),)),
                pltpu.SemaphoreType.DMA((sum(counts),)),
            ],
        ),
        out_shape=jax.ShapeDtypeStruct(query_grad.shape, query_grad.dtype),
        input_output_aliases={1: 0},
        cost_estimate=COST,
    )(where, query_grad, *parts)


NT = (((1,), (1,)), ((), ()))
NN = (((1,), (0,)), ((), ()))
TN = (((0,), (0,)), ((), ()))


def dot(a, b, dims):
    return lax.dot_general(a, b, dims, preferred_element_type=jnp.float32)


def attend_body(count, skipped, where_ref, *refs):
    latent_ref, rope_low_ref, rope_high_ref, bias_ref = refs[:4]
    q_ref, d_ref, twin_q_ref, twin_d_ref = refs[4:8]
    weights = refs[8 + skipped : 8 + skipped + 2 * count]
    at = 8 + skipped + 2 * count
    query_out, twin_out, latent_out, rope_out, mark_out = refs[at : at + 5]
    wk_ref, wv_ref, q_both, d_both, grad_both, dk_ref, dv_ref = refs[at + 5 :]
    step = pl.program_id(0)
    core = where_ref[0]

    for i in range(count):

        @pl.when(step == i)
        def _():
            wk_ref[...] = weights[2 * i][...]
            wv_ref[...] = weights[2 * i + 1][...]

    for own in range(2):

        @pl.when(core == own)
        def _():
            q_both[own] = q_ref[...]
            d_both[own] = d_ref[...]
            q_both[1 - own] = twin_q_ref[...]
            d_both[1 - own] = twin_d_ref[...]

    latent = latent_ref[...]
    keys = dot(latent, wk_ref[...], NN)
    values = dot(latent, wv_ref[...], NN).astype(jnp.bfloat16)
    low = lax.broadcasted_iota(jnp.int32, (ROWS, NOPE), 1) < ROPE
    rope_sum = jnp.zeros((ROWS, NOPE), jnp.float32)

    def fold(first, second):
        return jnp.concatenate(
            [first[:TOK], first[TOK:] + second[:WIN], second[WIN:]], axis=0
        )

    for pair in range(GROUP // 2):
        query_parts = [[], []]
        key_parts = []
        for odd in range(2):
            head = 2 * pair + odd
            key = keys[:, head * NOPE : (head + 1) * NOPE]
            if odd:
                turned = pltpu.roll(key, ROPE, 1)
                tiles = [
                    jnp.where(low, 0.0, turned).astype(jnp.bfloat16),
                    jnp.where(low, turned, rope_high_ref[...]).astype(jnp.bfloat16),
                ]
            else:
                tiles = [key.astype(jnp.bfloat16), rope_low_ref[...]]
            wide = jnp.concatenate(tiles, axis=1)
            value = values[:, head * VDIM : (head + 1) * VDIM]
            start = pair * 2 * (NOPE + ROPE) + odd * NOPE
            dk, dv = [], []
            for s in range(2):
                span = slice(s * TOK, s * TOK + SPAN)
                q = q_both[s, :, start : start + 2 * NOPE]
                d = d_both[s, :, head * VDIM : (head + 1) * VDIM]
                scores = dot(wide[span], q, NT) * SCALE + bias_ref[s]
                shifted = jnp.exp(scores - jnp.max(scores, axis=0, keepdims=True))
                inverse = 1.0 / jnp.sum(shifted, axis=0, keepdims=True)
                prob_grad = dot(value[span], d, NT)
                probs = shifted * inverse
                delta = jnp.sum(probs * prob_grad, axis=0, keepdims=True)
                score_grad = (SCALE * probs * (prob_grad - delta)).astype(jnp.bfloat16)
                probs_low = probs.astype(jnp.bfloat16)
                query_parts[s].append(dot(score_grad, wide[span], TN))
                dk.append(dot(score_grad, q, NN))
                dv.append(dot(probs_low, d, NN))
            dv_ref[:, head * VDIM : (head + 1) * VDIM] = fold(*dv).astype(jnp.bfloat16)
            key_parts.append(fold(*dk))
        even, odd = key_parts
        dk_ref[:, 2 * pair * NOPE : (2 * pair + 1) * NOPE] = even[:, :NOPE].astype(jnp.bfloat16)
        dk_ref[:, (2 * pair + 1) * NOPE : (2 * pair + 2) * NOPE] = pltpu.roll(
            jnp.where(low, odd[:, NOPE:], odd[:, :NOPE]), ROPE, 1
        ).astype(jnp.bfloat16)
        rope_sum = rope_sum + jnp.where(low, even[:, NOPE:], odd[:, NOPE:])
        for s in range(2):
            first, second = query_parts[s]
            left = pair * 3 * NOPE
            grad_both[s, :, left : left + NOPE] = first[:, :NOPE].astype(jnp.bfloat16)
            grad_both[s, :, left + NOPE : left + 2 * NOPE] = (
                first[:, NOPE:] + second[:, :NOPE]
            ).astype(jnp.bfloat16)
            grad_both[s, :, left + 2 * NOPE : left + 3 * NOPE] = second[:, NOPE:].astype(
                jnp.bfloat16
            )

    latent_sum = dot(dk_ref[...], wk_ref[...], NT) + dot(dv_ref[...], wv_ref[...], NT)

    @pl.when(step == 0)
    def _():
        latent_out[...] = latent_sum
        rope_out[...] = rope_sum
        mark_out[...] = jnp.zeros_like(mark_out)

    @pl.when(step > 0)
    def _():
        latent_out[...] += latent_sum
        rope_out[...] += rope_sum

    for own in range(2):

        @pl.when(core == own)
        def _():
            query_out[...] = grad_both[own]
            twin_out[0] = grad_both[1 - own]


def attend(
    where, shared, query, out_grad, twin_query, twin_grad, query_grad, weights, after=(), heavy=1
):
    count = len(weights)
    chained = query_grad is not None
    skipped = ([query_grad] if chained else []) + list(after)
    head_block = lambda width: pl.BlockSpec((TOK, width), lambda g, w: (0, 2 * w[1 + g] + w[0]))
    whole = lambda shape: pl.BlockSpec(shape, lambda g, w: (0,) * len(shape))
    in_specs = [
        whole((ROWS, LATENT)),
        whole((ROWS, NOPE)),
        whole((ROWS, NOPE)),
        whole((2, SPAN, TOK)),
        head_block(QW),
        head_block(VW),
        head_block(QW),
        head_block(VW),
    ]
    operands = [where, *shared, query, out_grad, twin_query, twin_grad, *skipped]
    in_specs += [pl.BlockSpec(memory_space=pl.ANY)] * len(skipped)
    for (key_part, key_at), (value_part, value_at) in weights:
        in_specs.append(pl.BlockSpec((LATENT, VW), lambda g, w, at=key_at: (at, 0)))
        in_specs.append(pl.BlockSpec((LATENT, VW), lambda g, w, at=value_at: (at, 0)))
        operands += [key_part, value_part]
    return pl.pallas_call(
        functools.partial(attend_body, count, len(skipped)),
        grid_spec=pltpu.PrefetchScalarGridSpec(
            num_scalar_prefetch=1,
            grid=(count,),
            in_specs=in_specs,
            out_specs=[
                head_block(QW),
                pl.BlockSpec((1, TOK, QW), lambda g, w: (g, 0, 0)),
                whole((ROWS, LATENT)),
                whole((ROWS, NOPE)),
                whole((8, NOPE)),
            ],
            scratch_shapes=[
                pltpu.VMEM((LATENT, VW), jnp.bfloat16),
                pltpu.VMEM((LATENT, VW), jnp.bfloat16),
                pltpu.VMEM((2, TOK, QW), jnp.bfloat16),
                pltpu.VMEM((2, TOK, VW), jnp.bfloat16),
                pltpu.VMEM((2, TOK, QW), jnp.bfloat16),
                pltpu.VMEM((ROWS, VW), jnp.bfloat16),
                pltpu.VMEM((ROWS, VW), jnp.bfloat16),
            ],
        ),
        out_shape=[
            jax.ShapeDtypeStruct((TOK, HEADS * (NOPE + ROPE)), jnp.bfloat16),
            jax.ShapeDtypeStruct((count, TOK, QW), jnp.bfloat16),
            jax.ShapeDtypeStruct((ROWS, LATENT), jnp.float32),
            jax.ShapeDtypeStruct((ROWS, NOPE), jnp.float32),
            jax.ShapeDtypeStruct((8, NOPE), jnp.float32),
        ],
        input_output_aliases={9: 0} if chained else {},
        compiler_params=pltpu.CompilerParams(vmem_limit_bytes=60 * 1024 * 1024),
        cost_estimate=pl.CostEstimate(
            flops=heavy * count * 500_000_000, bytes_accessed=count * 500_000, transcendentals=0
        ),
    )(*operands)


def local(
    query,
    out_grad,
    latent,
    rope_key,
    w_key,
    w_value,
    grad_stream,
    expert_ids,
    gate_weights,
    saved_hidden,
    w_down,
):
    query, out_grad, latent, rope_key = query[0], out_grad[0], latent[0], rope_key[0]
    grad_stream, expert_ids, gate_weights = grad_stream[0], expert_ids[0], gate_weights[0]
    index = lax.axis_index("ctx")
    core = index % 2
    chip = index // 2
    x = chip // 2
    half = chip % 2

    def group(step, flip):
        return 2 * ((x + step) % 4) + (half ^ flip)

    def spots(*groups):
        return jnp.stack([core, *groups]).astype(jnp.int32)

    def both(stack):
        return ((stack, 0), (stack, 1))

    mine = jnp.concatenate([latent, rope_key], axis=1)
    twin_rows = lax.ppermute(mine, "ctx", TWIN)
    chip_rows = jnp.where(
        core == 0,
        jnp.concatenate([mine, twin_rows], axis=0),
        jnp.concatenate([twin_rows, mine], axis=0),
    )
    halo = lax.ppermute(
        chip_rows[2 * TOK - WIN :], "ctx", [(i, i + 2) for i in range(CTX - 2)]
    )
    own = stack(w_key, w_value)
    before = lax.ppermute(own, "ctx", RIGHT)
    after = lax.ppermute(own, "ctx", LEFT)
    beside = lax.ppermute(own, ("ctx", "exp"), ACROSS)
    twin_query = lax.ppermute(query, "ctx", TWIN)
    twin_grad = lax.ppermute(out_grad, "ctx", TWIN)
    down = w_down[0]
    other_down = lax.ppermute(down, "ctx", [(i, i ^ 2) for i in range(CTX)])
    down = jnp.where(
        half == 0,
        jnp.concatenate([down, other_down], axis=1),
        jnp.concatenate([other_down, down], axis=1),
    )

    share = EXPERTS // EXP
    slots = jnp.arange(EXP * CAP, dtype=jnp.int32)[None, :]
    ids = tie(expert_ids, halo)
    match = [ids[:, k : k + 1] == slots // CAP * share for k in range(TOPK)]
    live = functools.reduce(jnp.logical_or, match)
    token_at = jnp.arange(TOK, dtype=jnp.int32)
    earlier = dot(
        (token_at[:, None] > token_at[None, :]).astype(jnp.bfloat16), live.astype(jnp.bfloat16), NN
    )
    token_hot = (live & (earlier == (slots % CAP).astype(jnp.float32))).astype(jnp.bfloat16)
    gates = sum(
        jnp.where(match[k], gate_weights[:, k : k + 1].astype(jnp.float32), 0.0)
        for k in range(TOPK)
    )
    gate_send = jnp.sum(token_hot.astype(jnp.float32) * gates, axis=0).reshape(EXP, 1, CAP)
    outbound = dot(token_hot, grad_stream, TN).astype(jnp.bfloat16)
    tiles = outbound.shape[1] // NOPE
    outbound = jnp.concatenate(
        [
            outbound.reshape(EXP, CAP * tiles, NOPE),
            jnp.pad(gate_send.astype(jnp.bfloat16), ((0, 0), (0, 7), (0, NOPE - CAP))),
        ],
        axis=1,
    )
    outbound = tie(outbound, twin_query, own)
    routed = lax.all_to_all(outbound, "exp", split_axis=0, concat_axis=0, tiled=True)

    rows = jnp.concatenate([halo, chip_rows], axis=0)
    rope_rows = rows[:, LATENT:]
    blank = jnp.zeros_like(rope_rows)
    key_at = jnp.arange(SPAN, dtype=jnp.int32)[:, None]
    query_at = jnp.arange(TOK, dtype=jnp.int32)[None, :]
    inside = (key_at > query_at) & (key_at <= query_at + WIN)
    first = inside & ((chip > 0) | (key_at >= WIN))
    shared = (
        rows[:, :LATENT],
        jnp.concatenate([rope_rows, blank], axis=1),
        jnp.concatenate([blank, rope_rows], axis=1).astype(jnp.float32),
        jnp.where(jnp.stack([first, inside]), 0.0, -jnp.inf).astype(jnp.float32),
    )
    common = (shared, query, out_grad, twin_query, twin_grad)

    where_a = spots(group(0, 0))
    query_grad, part_a, latent_a, rope_a, mark_a = attend(where_a, *common, None, [both(own)])

    opposite = lax.ppermute(before, "ctx", RIGHT)
    beside_after = lax.ppermute(beside, "ctx", LEFT)
    beside_before = lax.ppermute(before, ("ctx", "exp"), ACROSS)
    where_b = spots(group(-1, 0), group(1, 0), group(0, 1))
    query_grad, part_b, latent_b, rope_b, mark_b = attend(
        where_b, *common, query_grad, [both(before), both(after), both(beside)], heavy=10
    )
    routed = tie(routed, mark_b)
    row_gate = routed[:, CAP * tiles, :CAP].reshape(EXP * CAP, 1)
    slices = routed[:, : CAP * tiles].reshape(EXP * CAP, 4, 2, 2, -1)
    slices = slices.transpose(1, 3, 0, 2, 4).reshape(CHIPS, EXP * CAP, -1)
    slices = lax.all_to_all(
        slices, "ctx", split_axis=0, concat_axis=0, tiled=True, axis_index_groups=RING
    )

    part_a = lax.ppermute(part_a, "ctx", TWIN)
    part_b = lax.ppermute(part_b, "ctx", TWIN)

    last_key = lax.ppermute(tie(beside_after[:LATENT], mark_b), "ctx", LEFT)
    last_value = lax.ppermute(tie(opposite[LATENT:], mark_b), ("ctx", "exp"), ACROSS)
    where_c = spots(group(2, 0), group(-1, 1))
    query_grad, part_c, latent_c, rope_c, mark_c = attend(
        where_c, *common, query_grad, [both(opposite), both(beside_before)], (mark_b,)
    )
    part_c = lax.ppermute(part_c, "ctx", TWIN)

    slices = tie(slices, mark_c).reshape(4, 2, EXP * CAP, -1)

    def terms(number):
        rows = lax.dynamic_index_in_dim(slices, number, 1, keepdims=False)
        rows = rows.reshape(4 * EXP * CAP, -1)
        return dot(rows, down, NT).astype(jnp.bfloat16).reshape(4, EXP * CAP, FFH)

    give = terms(1 - core)
    keep = terms(core)
    taken = lax.ppermute(give, "ctx", TWIN)

    keep = (keep.astype(jnp.float32) + taken.astype(jnp.float32)).astype(jnp.bfloat16)
    pieces = lax.all_to_all(
        keep, "ctx", split_axis=0, concat_axis=0, tiled=True, axis_index_groups=RING_CORE
    )

    where_d = spots(group(1, 1), group(2, 1))
    query_grad, part_d, latent_d, rope_d, mark_d = attend(
        where_d,
        *common,
        query_grad,
        [both(beside_after), ((last_key, 0), (last_value, 0))],
        (keep,),
    )
    part_d = lax.ppermute(part_d, "ctx", TWIN)
    rope_sum = rope_a + rope_b + rope_c + rope_d
    sums = jnp.concatenate(
        [latent_a + latent_b + latent_c + latent_d, rope_sum[:, :ROPE] + rope_sum[:, ROPE:]], axis=1
    )
    back = lax.ppermute(sums[:WIN], "ctx", [(i + 2, i) for i in range(CTX - 2)])
    low = sums[WIN : WIN + TOK]
    high = sums[WIN + TOK :]
    high = jnp.concatenate([high[: TOK - WIN], high[TOK - WIN :] + back], axis=0)
    kept = jnp.where(core == 0, low, high)
    given = lax.ppermute(jnp.where(core == 0, high, low), "ctx", TWIN)
    total = (kept + given).astype(jnp.bfloat16)
    query_grad = place(
        jnp.concatenate([where_a, where_b[1:], where_c[1:], where_d[1:]]),
        query_grad,
        (part_a, part_b, part_c, part_d),
    )

    raw_grad = jnp.sum(pieces.astype(jnp.float32), axis=0)
    gate_part = jnp.sum(saved_hidden[0, 0].astype(jnp.float32) * raw_grad, axis=1)
    hidden_grad = (row_gate.astype(jnp.float32) * raw_grad).astype(jnp.bfloat16)
    returned = lax.all_to_all(
        gate_part.reshape(EXP, CAP), "exp", split_axis=0, concat_axis=0, tiled=True
    )
    found = token_hot.astype(jnp.float32) * returned.reshape(1, -1)
    gate_grad = jnp.stack(
        [jnp.sum(jnp.where(match[k], found, 0.0), axis=1) for k in range(TOPK)], axis=1
    )
    return (
        query_grad[None],
        total[None, :, :LATENT],
        total[None, :, LATENT:],
        hidden_grad[None, None],
        gate_grad[None],
    )


def solution(mesh):
    in_specs = (
        P("exp", "ctx", None),
        P("exp", "ctx", None),
        P("exp", "ctx", None),
        P("exp", "ctx", None),
        P(None, "ctx"),
        P(None, "ctx"),
        P("exp", "ctx", None),
        P("exp", "ctx", None),
        P("exp", "ctx", None),
        P("ctx", "exp", None, None),
        P("exp", None, "ctx"),
    )
    out_specs = (
        P("exp", "ctx", None),
        P("exp", "ctx", None),
        P("exp", "ctx", None),
        P("ctx", "exp", None, None),
        P("exp", "ctx", None),
    )
    return jax.shard_map(local, mesh=mesh, in_specs=in_specs, out_specs=out_specs, check_vma=False)
```

```python
import functools

import jax
import jax.numpy as jnp
from jax import lax
from jax.experimental import pallas as pl
from jax.experimental.pallas import tpu as pltpu
from jax.sharding import PartitionSpec as P

HEADS = 64
NOPE = 128
ROPE = 64
VDIM = 128
LATENT = 512
FFH = 1536
EXPERTS = 160
TOPK = 6
WIN = 32
CAP = 6
CTX = 16
EXP = 16
TOK = 128
CHIPS = 8
GROUP = 4
QW = GROUP * (NOPE + ROPE)
VW = GROUP * VDIM
ROWS = 2 * TOK + WIN
SPAN = TOK + WIN
SCALE = (NOPE + ROPE) ** (-0.5)
CHIP_AT, HALF_AT = 9, 10
COST = pl.CostEstimate(flops=1_000_000, bytes_accessed=1_000_000, transcendentals=0)


def ctx_at(x, half, core):
    return ((x % 4) * 2 + half) * 2 + core


def ctx_moves(step):
    return [
        (ctx_at(x, half, core), ctx_at(x + step, half, core))
        for x in range(4)
        for half in range(2)
        for core in range(2)
    ]


RIGHT = ctx_moves(1)
LEFT = ctx_moves(-1)
TWIN = [(i, i ^ 1) for i in range(CTX)]
ACROSS = [
    ((i * EXP + e), ((i ^ 2) * EXP + (e ^ 8))) for i in range(CTX) for e in range(EXP)
]
RING = [[ctx_at(x, half, core) for x in range(4) for core in range(2)] for half in range(2)]
RING_CORE = [[ctx_at(x, half, core) for x in range(4)] for half in range(2) for core in range(2)]


def nothing_body(*refs):
    pass


def tie(value, *others):
    return pl.pallas_call(
        nothing_body,
        in_specs=[pl.BlockSpec(memory_space=pl.ANY)] * (1 + len(others)),
        out_specs=pl.BlockSpec(memory_space=pl.ANY),
        out_shape=jax.ShapeDtypeStruct(value.shape, value.dtype),
        input_output_aliases={0: 0},
        cost_estimate=COST,
    )(value, *others)


def stack_body(key_ref, value_ref, out_ref):
    out_ref[:LATENT] = key_ref[...]
    out_ref[LATENT:] = value_ref[...]


def stack(w_key, w_value):
    return pl.pallas_call(
        stack_body,
        out_shape=jax.ShapeDtypeStruct((2 * LATENT, VW), jnp.bfloat16),
        compiler_params=pltpu.CompilerParams(vmem_limit_bytes=60 * 1024 * 1024),
        cost_estimate=COST,
    )(w_key, w_value)


def join_body(latent_ref, rope_ref, out_ref):
    out_ref[:, :LATENT] = latent_ref[...]
    rope = rope_ref[...].astype(jnp.float32).T
    out_ref[:, LATENT:] = jnp.concatenate([rope, jnp.zeros_like(rope)], axis=1).astype(jnp.bfloat16)


def join(latent, rope_turned):
    return pl.pallas_call(
        join_body,
        out_shape=jax.ShapeDtypeStruct((TOK, LATENT + NOPE), jnp.bfloat16),
        compiler_params=pltpu.CompilerParams(vmem_limit_bytes=60 * 1024 * 1024),
        cost_estimate=COST,
    )(latent, rope_turned)


def prepare_body(where_ref, mine_ref, twin_ref, halo_ref, latent_ref, low_ref, high_ref):
    core = where_ref[0]

    def put(at, ref):
        rows = pl.ds(at, ref.shape[0])
        latent_ref[rows, :] = ref[:, :LATENT]
        rope = ref[:, LATENT:]
        low_ref[rows, :] = rope
        high_ref[rows, :] = pltpu.roll(rope.astype(jnp.float32), ROPE, 1)

    put(0, halo_ref)
    for own in range(2):

        @pl.when(core == own)
        def _():
            put(WIN + own * TOK, mine_ref)
            put(WIN + (1 - own) * TOK, twin_ref)


def prepare(where, mine, twin_rows, halo):
    return pl.pallas_call(
        prepare_body,
        in_specs=[pl.BlockSpec(memory_space=pltpu.SMEM)]
        + [pl.BlockSpec(memory_space=pltpu.VMEM)] * 3,
        out_shape=[
            jax.ShapeDtypeStruct((ROWS, LATENT), jnp.bfloat16),
            jax.ShapeDtypeStruct((ROWS, NOPE), jnp.bfloat16),
            jax.ShapeDtypeStruct((ROWS, NOPE), jnp.float32),
        ],
        compiler_params=pltpu.CompilerParams(vmem_limit_bytes=60 * 1024 * 1024),
        cost_estimate=COST,
    )(where, mine, twin_rows, halo)


def place_body(counts, where_ref, grid_ref, after_ref, *refs):
    parts, out_ref = refs[: len(counts)], refs[len(counts)]
    held, in_sems, out_sems = refs[len(counts) + 1 :]
    core = where_ref[0]
    ways = []
    for part, count in zip(parts, counts):
        for i in range(count):
            at = len(ways)
            column = pl.multiple_of((2 * where_ref[1 + at] + 1 - core) * QW, QW)
            ways.append(
                (
                    pltpu.make_async_copy(part.at[i], held.at[at], in_sems.at[at]),
                    pltpu.make_async_copy(
                        held.at[at], out_ref.at[:, pl.ds(column, QW)], out_sems.at[at]
                    ),
                )
            )
    for arrive, _ in ways:
        arrive.start()
    for arrive, leave in ways:
        arrive.wait()
        leave.start()
    for _, leave in ways:
        leave.wait()


def place(where, query_grad, parts, after):
    counts = tuple(part.shape[0] for part in parts)
    return pl.pallas_call(
        functools.partial(place_body, counts),
        grid_spec=pltpu.PrefetchScalarGridSpec(
            num_scalar_prefetch=1,
            grid=(),
            in_specs=[pl.BlockSpec(memory_space=pl.ANY)] * (2 + len(parts)),
            out_specs=pl.BlockSpec(memory_space=pl.ANY),
            scratch_shapes=[
                pltpu.VMEM((sum(counts), TOK, QW), jnp.bfloat16),
                pltpu.SemaphoreType.DMA((sum(counts),)),
                pltpu.SemaphoreType.DMA((sum(counts),)),
            ],
        ),
        out_shape=jax.ShapeDtypeStruct(query_grad.shape, query_grad.dtype),
        input_output_aliases={1: 0},
        cost_estimate=COST,
    )(where, query_grad, after, *parts)


NT = (((1,), (1,)), ((), ()))
NN = (((1,), (0,)), ((), ()))
TN = (((0,), (0,)), ((), ()))


def dot(a, b, dims):
    return lax.dot_general(a, b, dims, preferred_element_type=jnp.float32)


def attend_body(count, base, skipped, where_ref, *refs):
    latent_ref, rope_low_ref, rope_high_ref = refs[:3]
    q_ref, d_ref, twin_q_ref, twin_d_ref = refs[3:7]
    weights = refs[7 + skipped : 7 + skipped + 2 * count]
    at = 7 + skipped + 2 * count
    sums = refs[at : at + 2] if skipped else ()
    at += len(sums)
    query_out, twin_out, latent_out, rope_out, mark_out = refs[at : at + 5]
    wk_ref, wv_ref, q_both, d_both, grad_both, dk_ref, dv_ref = refs[at + 5 :]
    step = pl.program_id(0)
    core = where_ref[0]
    key_at = lax.broadcasted_iota(jnp.int32, (SPAN, TOK), 0)
    query_at = lax.broadcasted_iota(jnp.int32, (SPAN, TOK), 1)
    inside = (key_at > query_at) & (key_at <= query_at + WIN)
    started = key_at >= jnp.where(where_ref[CHIP_AT] > 0, 0, WIN)
    masks = (inside & started, inside)

    for i in range(count):

        @pl.when(step == i)
        def _():
            wk_ref[...] = weights[2 * i][...]
            wv_ref[...] = weights[2 * i + 1][...]

    for own in range(2):

        @pl.when(core == own)
        def _():
            q_both[own] = q_ref[...]
            d_both[own] = d_ref[...]
            q_both[1 - own] = twin_q_ref[...]
            d_both[1 - own] = twin_d_ref[...]

    latent = latent_ref[...]
    keys = dot(latent, wk_ref[...], NN)
    values = dot(latent, wv_ref[...], NN).astype(jnp.bfloat16)
    low = lax.broadcasted_iota(jnp.int32, (ROWS, NOPE), 1) < ROPE
    rope_sum = jnp.zeros((ROWS, NOPE), jnp.float32)

    def fold(first, second):
        return jnp.concatenate(
            [first[:TOK], first[TOK:] + second[:WIN], second[WIN:]], axis=0
        )

    for pair in range(GROUP // 2):
        query_parts = [[], []]
        key_parts = []
        for odd in range(2):
            head = 2 * pair + odd
            key = keys[:, head * NOPE : (head + 1) * NOPE]
            if odd:
                turned = pltpu.roll(key, ROPE, 1)
                tiles = [
                    jnp.where(low, 0.0, turned).astype(jnp.bfloat16),
                    jnp.where(low, turned, rope_high_ref[...]).astype(jnp.bfloat16),
                ]
            else:
                tiles = [key.astype(jnp.bfloat16), rope_low_ref[...]]
            wide = jnp.concatenate(tiles, axis=1)
            value = values[:, head * VDIM : (head + 1) * VDIM]
            start = pair * 2 * (NOPE + ROPE) + odd * NOPE
            dk, dv = [], []
            for s in range(2):
                span = slice(s * TOK, s * TOK + SPAN)
                q = q_both[s, :, start : start + 2 * NOPE]
                d = d_both[s, :, head * VDIM : (head + 1) * VDIM]
                scores = jnp.where(masks[s], dot(wide[span], q, NT) * SCALE, -jnp.inf)
                shifted = jnp.exp(scores - jnp.max(scores, axis=0, keepdims=True))
                inverse = 1.0 / jnp.sum(shifted, axis=0, keepdims=True)
                prob_grad = dot(value[span], d, NT)
                probs = shifted * inverse
                delta = jnp.sum(probs * prob_grad, axis=0, keepdims=True)
                score_grad = (SCALE * probs * (prob_grad - delta)).astype(jnp.bfloat16)
                probs_low = probs.astype(jnp.bfloat16)
                query_parts[s].append(dot(score_grad, wide[span], TN))
                dk.append(dot(score_grad, q, NN))
                dv.append(dot(probs_low, d, NN))
            dv_ref[:, head * VDIM : (head + 1) * VDIM] = fold(*dv).astype(jnp.bfloat16)
            key_parts.append(fold(*dk))
        even, odd = key_parts
        dk_ref[:, 2 * pair * NOPE : (2 * pair + 1) * NOPE] = even[:, :NOPE].astype(jnp.bfloat16)
        dk_ref[:, (2 * pair + 1) * NOPE : (2 * pair + 2) * NOPE] = pltpu.roll(
            jnp.where(low, odd[:, NOPE:], odd[:, :NOPE]), ROPE, 1
        ).astype(jnp.bfloat16)
        rope_sum = rope_sum + jnp.where(low, even[:, NOPE:], odd[:, NOPE:])
        for s in range(2):
            first, second = query_parts[s]
            left = pair * 3 * NOPE
            grad_both[s, :, left : left + NOPE] = first[:, :NOPE].astype(jnp.bfloat16)
            grad_both[s, :, left + NOPE : left + 2 * NOPE] = (
                first[:, NOPE:] + second[:, :NOPE]
            ).astype(jnp.bfloat16)
            grad_both[s, :, left + 2 * NOPE : left + 3 * NOPE] = second[:, NOPE:].astype(
                jnp.bfloat16
            )

    latent_sum = dot(dk_ref[...], wk_ref[...], NT) + dot(dv_ref[...], wv_ref[...], NT)

    @pl.when(step == 0)
    def _():
        latent_out[...] = sums[0][...] + latent_sum if sums else latent_sum
        rope_out[...] = sums[1][...] + rope_sum if sums else rope_sum
        mark_out[...] = jnp.zeros_like(mark_out)

    @pl.when(step > 0)
    def _():
        latent_out[...] += latent_sum
        rope_out[...] += rope_sum

    for own in range(2):

        @pl.when(core == own)
        def _():
            query_out[...] = grad_both[own]
            twin_out[0] = grad_both[1 - own]


def attend(
    where, base, shared, query, out_grad, twin_query, twin_grad, weights, earlier=(), after=(), heavy=1
):
    count = len(weights)
    skipped = list(earlier[:1]) + list(after)
    head_block = lambda width: pl.BlockSpec((TOK, width), lambda g, w: (0, 2 * w[base + g] + w[0]))
    whole = lambda shape: pl.BlockSpec(shape, lambda g, w: (0,) * len(shape))
    in_specs = [
        whole((ROWS, LATENT)),
        whole((ROWS, NOPE)),
        whole((ROWS, NOPE)),
        head_block(QW),
        head_block(VW),
        head_block(QW),
        head_block(VW),
    ]
    operands = [where, *shared, query, out_grad, twin_query, twin_grad, *skipped]
    in_specs += [pl.BlockSpec(memory_space=pl.ANY)] * len(skipped)
    for (key_part, key_at), (value_part, value_at) in weights:
        in_specs.append(pl.BlockSpec((LATENT, VW), lambda g, w, at=key_at: (at, 0)))
        in_specs.append(pl.BlockSpec((LATENT, VW), lambda g, w, at=value_at: (at, 0)))
        operands += [key_part, value_part]
    if earlier:
        in_specs += [whole((ROWS, LATENT)), whole((ROWS, NOPE))]
        operands += earlier[1:]
    query_grad, part, latent_sum, rope_sum, mark = pl.pallas_call(
        functools.partial(attend_body, count, base, len(skipped)),
        grid_spec=pltpu.PrefetchScalarGridSpec(
            num_scalar_prefetch=1,
            grid=(count,),
            in_specs=in_specs,
            out_specs=[
                head_block(QW),
                pl.BlockSpec((1, TOK, QW), lambda g, w: (g, 0, 0)),
                whole((ROWS, LATENT)),
                whole((ROWS, NOPE)),
                whole((8, NOPE)),
            ],
            scratch_shapes=[
                pltpu.VMEM((LATENT, VW), jnp.bfloat16),
                pltpu.VMEM((LATENT, VW), jnp.bfloat16),
                pltpu.VMEM((2, TOK, QW), jnp.bfloat16),
                pltpu.VMEM((2, TOK, VW), jnp.bfloat16),
                pltpu.VMEM((2, TOK, QW), jnp.bfloat16),
                pltpu.VMEM((ROWS, VW), jnp.bfloat16),
                pltpu.VMEM((ROWS, VW), jnp.bfloat16),
            ],
        ),
        out_shape=[
            jax.ShapeDtypeStruct((TOK, HEADS * (NOPE + ROPE)), jnp.bfloat16),
            jax.ShapeDtypeStruct((count, TOK, QW), jnp.bfloat16),
            jax.ShapeDtypeStruct((ROWS, LATENT), jnp.float32),
            jax.ShapeDtypeStruct((ROWS, NOPE), jnp.float32),
            jax.ShapeDtypeStruct((8, NOPE), jnp.float32),
        ],
        input_output_aliases={8: 0} if earlier else {},
        compiler_params=pltpu.CompilerParams(vmem_limit_bytes=60 * 1024 * 1024),
        cost_estimate=pl.CostEstimate(
            flops=heavy * count * 500_000_000, bytes_accessed=count * 500_000, transcendentals=0
        ),
    )(*operands)
    return query_grad, latent_sum, rope_sum, part, mark


def terms_body(where_ref, rows_ref, own_ref, other_ref, *refs):
    out_ref = refs[-1]
    here = where_ref[HALF_AT] * (EXP * CAP)
    there = (1 - where_ref[HALF_AT]) * (EXP * CAP)

    def rows(at):
        part = rows_ref[:, 0, pl.ds(pl.multiple_of(at, EXP * CAP), EXP * CAP), :]
        return part.reshape(4 * EXP * CAP, -1)

    total = dot(rows(here), own_ref[...], NN) + dot(rows(there), other_ref[...], NN)
    out_ref[...] = total.astype(jnp.bfloat16).reshape(out_ref.shape)


def terms(where, twin, slices, own_down, other_down, after):
    rows = slices.reshape(4, 2, 2 * EXP * CAP, -1)
    depth = rows.shape[3]
    weight = pl.BlockSpec((depth, FFH), lambda g, w: (0, 0))
    number = (lambda w: 1 - w[0]) if twin else (lambda w: w[0])
    return pl.pallas_call(
        terms_body,
        grid_spec=pltpu.PrefetchScalarGridSpec(
            num_scalar_prefetch=1,
            grid=(1,),
            in_specs=[
                pl.BlockSpec(
                    (4, 1, 2 * EXP * CAP, depth), lambda g, w: (0, number(w), 0, 0)
                ),
                weight,
                weight,
            ]
            + [pl.BlockSpec(memory_space=pl.ANY)] * len(after),
            out_specs=pl.BlockSpec((4, EXP * CAP, FFH), lambda g, w: (0, 0, 0)),
        ),
        out_shape=jax.ShapeDtypeStruct((4, EXP * CAP, FFH), jnp.bfloat16),
        compiler_params=pltpu.CompilerParams(vmem_limit_bytes=60 * 1024 * 1024),
        cost_estimate=pl.CostEstimate(
            flops=100_000_000, bytes_accessed=100_000, transcendentals=0
        ),
    )(where, rows, own_down, other_down, *after)


def local(
    query,
    out_grad,
    latent,
    rope_key,
    w_key,
    w_value,
    grad_stream,
    expert_ids,
    gate_weights,
    saved_hidden,
    w_down,
):
    query, out_grad, latent, rope_key = query[0], out_grad[0], latent[0], rope_key[0]
    grad_stream, expert_ids, gate_weights = grad_stream[0], expert_ids[0], gate_weights[0]
    index = lax.axis_index("ctx")
    core = index % 2
    chip = index // 2
    x = chip // 2
    half = chip % 2

    def group(step, flip):
        return 2 * ((x + step) % 4) + (half ^ flip)

    groups = [
        group(0, 0),
        group(-1, 0),
        group(1, 0),
        group(0, 1),
        group(2, 0),
        group(-1, 1),
        group(1, 1),
        group(2, 1),
    ]
    where = jnp.stack([core, *groups, chip, half]).astype(jnp.int32)

    def both(stack):
        return ((stack, 0), (stack, 1))

    mine = join(latent, rope_key.T)
    twin_rows = lax.ppermute(mine, "ctx", TWIN)
    halo = lax.ppermute(
        jnp.where(core == 0, twin_rows[TOK - WIN :], mine[TOK - WIN :]), "ctx", [(i, i + 2) for i in range(CTX - 2)]
    )
    own = stack(w_key, w_value)
    before = lax.ppermute(own, "ctx", RIGHT)
    after = lax.ppermute(own, "ctx", LEFT)
    beside = lax.ppermute(own, ("ctx", "exp"), ACROSS)
    twin_query = lax.ppermute(query, "ctx", TWIN)
    twin_grad = lax.ppermute(out_grad, "ctx", TWIN)
    down = w_down[0].T
    other_down = lax.ppermute(down, "ctx", [(i, i ^ 2) for i in range(CTX)])

    share = EXPERTS // EXP
    slots = jnp.arange(EXP * CAP, dtype=jnp.int32)[None, :]
    ids = tie(expert_ids, own)
    match = [ids[:, k : k + 1] == slots // CAP * share for k in range(TOPK)]
    live = functools.reduce(jnp.logical_or, match)
    token_at = jnp.arange(TOK, dtype=jnp.int32)
    earlier = dot(
        (token_at[:, None] > token_at[None, :]).astype(jnp.bfloat16), live.astype(jnp.bfloat16), NN
    )
    token_hot = (live & (earlier == (slots % CAP).astype(jnp.float32))).astype(jnp.bfloat16)
    gates = sum(
        jnp.where(match[k], gate_weights[:, k : k + 1].astype(jnp.float32), 0.0)
        for k in range(TOPK)
    )
    gate_send = jnp.sum(token_hot.astype(jnp.float32) * gates, axis=0).reshape(EXP, 1, CAP)
    outbound = dot(token_hot, grad_stream, TN).astype(jnp.bfloat16)
    tiles = outbound.shape[1] // NOPE
    outbound = jnp.concatenate(
        [
            outbound.reshape(EXP, CAP * tiles, NOPE),
            jnp.pad(gate_send.astype(jnp.bfloat16), ((0, 0), (0, 7), (0, NOPE - CAP))),
        ],
        axis=1,
    )
    outbound = tie(outbound, twin_query, own)
    routed = lax.all_to_all(outbound, "exp", split_axis=0, concat_axis=0, tiled=True)

    shared = prepare(where, mine, twin_rows, halo)
    common = (shared, query, out_grad, twin_query, twin_grad)

    *sums, part_a, mark_a = attend(where, 1, *common, [both(own)])

    opposite = lax.ppermute(before, "ctx", RIGHT)
    beside_after = lax.ppermute(beside, "ctx", LEFT)
    beside_before = lax.ppermute(before, ("ctx", "exp"), ACROSS)
    *sums, part_b, mark_b = attend(
        where, 2, *common, [both(before), both(after), both(beside)], sums, heavy=10
    )
    routed = tie(routed, mark_b, other_down)
    row_gate = routed[:, CAP * tiles, :CAP].reshape(EXP * CAP, 1)
    slices = routed[:, : CAP * tiles].reshape(EXP * CAP, 4, 2, 2, -1)
    slices = slices.transpose(1, 3, 2, 0, 4).reshape(CHIPS, 2 * EXP * CAP, -1)
    slices = lax.all_to_all(
        slices, "ctx", split_axis=0, concat_axis=0, tiled=True, axis_index_groups=RING
    )

    part_a = lax.ppermute(part_a, "ctx", TWIN)
    part_b = lax.ppermute(part_b, "ctx", TWIN)

    key_half = tie(beside_after[:LATENT], mark_b)
    value_half = tie(opposite[LATENT:], mark_b)
    last_key = lax.ppermute(key_half, "ctx", LEFT)
    last_value = lax.ppermute(value_half, ("ctx", "exp"), ACROSS)

    give = terms(
        where, True, slices, down, other_down, (mark_b, beside_before, key_half, value_half)
    )
    keep = terms(where, False, slices, down, other_down, (give,))
    taken = lax.ppermute(give, "ctx", TWIN)

    keep = (keep.astype(jnp.float32) + taken.astype(jnp.float32)).astype(jnp.bfloat16)
    pieces = lax.all_to_all(
        keep, "ctx", split_axis=0, concat_axis=0, tiled=True, axis_index_groups=RING_CORE
    )

    *sums, part_c, mark_c = attend(
        where,
        5,
        *common,
        [
            both(opposite),
            both(beside_before),
            both(beside_after),
            ((last_key, 0), (last_value, 0)),
        ],
        sums,
        (keep,),
    )
    part_c = lax.ppermute(part_c, "ctx", TWIN)

    query_grad, latent_sum, rope_sum = sums
    latent_sum = tie(latent_sum, pieces)
    sums = jnp.concatenate([latent_sum, rope_sum[:, :ROPE] + rope_sum[:, ROPE:]], axis=1)
    back = lax.ppermute(sums[:WIN], "ctx", [(i + 2, i) for i in range(CTX - 2)])
    low = sums[WIN : WIN + TOK]
    high = sums[WIN + TOK :]
    high = jnp.concatenate([high[: TOK - WIN], high[TOK - WIN :] + back], axis=0)
    kept = jnp.where(core == 0, low, high)
    given = lax.ppermute(jnp.where(core == 0, high, low), "ctx", TWIN)
    total = (kept + given).astype(jnp.bfloat16)
    raw_grad = jnp.sum(pieces.astype(jnp.float32), axis=0)
    gate_part = jnp.sum(saved_hidden[0, 0].astype(jnp.float32) * raw_grad, axis=1)
    hidden_grad = (row_gate.astype(jnp.float32) * raw_grad).astype(jnp.bfloat16)
    returned = lax.all_to_all(
        gate_part.reshape(EXP, CAP), "exp", split_axis=0, concat_axis=0, tiled=True
    )
    query_grad = place(where, query_grad, (part_a, part_b, part_c), gate_part[None])
    found = token_hot.astype(jnp.float32) * returned.reshape(1, -1)
    gate_grad = jnp.stack(
        [jnp.sum(jnp.where(match[k], found, 0.0), axis=1) for k in range(TOPK)], axis=1
    )
    return (
        query_grad[None],
        total[None, :, :LATENT],
        total[None, :, LATENT:],
        hidden_grad[None, None],
        gate_grad[None],
    )


def solution(mesh):
    in_specs = (
        P("exp", "ctx", None),
        P("exp", "ctx", None),
        P("exp", "ctx", None),
        P("exp", "ctx", None),
        P(None, "ctx"),
        P(None, "ctx"),
        P("exp", "ctx", None),
        P("exp", "ctx", None),
        P("exp", "ctx", None),
        P("ctx", "exp", None, None),
        P("exp", None, "ctx"),
    )
    out_specs = (
        P("exp", "ctx", None),
        P("exp", "ctx", None),
        P("exp", "ctx", None),
        P("ctx", "exp", None, None),
        P("exp", "ctx", None),
    )
    return jax.shard_map(local, mesh=mesh, in_specs=in_specs, out_specs=out_specs, check_vma=False)
```

```python
import functools

import jax
import jax.numpy as jnp
from jax import lax
from jax.experimental import pallas as pl
from jax.experimental.pallas import tpu as pltpu
from jax.sharding import PartitionSpec as P

HEADS = 64
NOPE = 128
ROPE = 64
VDIM = 128
LATENT = 512
FFH = 1536
EXPERTS = 160
TOPK = 6
WIN = 32
CAP = 6
CTX = 16
EXP = 16
TOK = 128
CHIPS = 8
GROUP = 4
QW = GROUP * (NOPE + ROPE)
VW = GROUP * VDIM
ROWS = 2 * TOK + WIN
SPAN = TOK + WIN
SCALE = (NOPE + ROPE) ** (-0.5)
CHIP_AT, HALF_AT = 9, 10
COST = pl.CostEstimate(flops=1_000_000, bytes_accessed=1_000_000, transcendentals=0)


def ctx_at(x, half, core):
    return ((x % 4) * 2 + half) * 2 + core


def ctx_moves(step):
    return [
        (ctx_at(x, half, core), ctx_at(x + step, half, core))
        for x in range(4)
        for half in range(2)
        for core in range(2)
    ]


RIGHT = ctx_moves(1)
LEFT = ctx_moves(-1)
TWIN = [(i, i ^ 1) for i in range(CTX)]
ACROSS = [
    ((i * EXP + e), ((i ^ 2) * EXP + (e ^ 8))) for i in range(CTX) for e in range(EXP)
]
RING = [[ctx_at(x, half, core) for x in range(4) for core in range(2)] for half in range(2)]
RING_CORE = [[ctx_at(x, half, core) for x in range(4)] for half in range(2) for core in range(2)]


def nothing_body(*refs):
    pass


def tie(value, *others):
    return pl.pallas_call(
        nothing_body,
        in_specs=[pl.BlockSpec(memory_space=pl.ANY)] * (1 + len(others)),
        out_specs=pl.BlockSpec(memory_space=pl.ANY),
        out_shape=jax.ShapeDtypeStruct(value.shape, value.dtype),
        input_output_aliases={0: 0},
        cost_estimate=COST,
    )(value, *others)


def stack_body(key_ref, value_ref, out_ref):
    out_ref[:LATENT] = key_ref[...]
    out_ref[LATENT:] = value_ref[...]


def stack(w_key, w_value):
    return pl.pallas_call(
        stack_body,
        out_shape=jax.ShapeDtypeStruct((2 * LATENT, VW), jnp.bfloat16),
        compiler_params=pltpu.CompilerParams(vmem_limit_bytes=60 * 1024 * 1024),
        cost_estimate=COST,
    )(w_key, w_value)


def join_body(latent_ref, rope_ref, out_ref):
    out_ref[:, :LATENT] = latent_ref[...]
    rope = rope_ref[...].astype(jnp.float32).T
    out_ref[:, LATENT:] = jnp.concatenate([rope, jnp.zeros_like(rope)], axis=1).astype(jnp.bfloat16)


def join(latent, rope_turned):
    return pl.pallas_call(
        join_body,
        out_shape=jax.ShapeDtypeStruct((TOK, LATENT + NOPE), jnp.bfloat16),
        compiler_params=pltpu.CompilerParams(vmem_limit_bytes=60 * 1024 * 1024),
        cost_estimate=COST,
    )(latent, rope_turned)


def prepare_body(where_ref, mine_ref, twin_ref, halo_ref, latent_ref, low_ref, high_ref):
    core = where_ref[0]

    def put(at, ref):
        rows = pl.ds(at, ref.shape[0])
        latent_ref[rows, :] = ref[:, :LATENT]
        rope = ref[:, LATENT:]
        low_ref[rows, :] = rope
        high_ref[rows, :] = pltpu.roll(rope.astype(jnp.float32), ROPE, 1)

    put(0, halo_ref)
    for own in range(2):

        @pl.when(core == own)
        def _():
            put(WIN + own * TOK, mine_ref)
            put(WIN + (1 - own) * TOK, twin_ref)


def prepare(where, mine, twin_rows, halo):
    return pl.pallas_call(
        prepare_body,
        in_specs=[pl.BlockSpec(memory_space=pltpu.SMEM)]
        + [pl.BlockSpec(memory_space=pltpu.VMEM)] * 3,
        out_shape=[
            jax.ShapeDtypeStruct((ROWS, LATENT), jnp.bfloat16),
            jax.ShapeDtypeStruct((ROWS, NOPE), jnp.bfloat16),
            jax.ShapeDtypeStruct((ROWS, NOPE), jnp.float32),
        ],
        compiler_params=pltpu.CompilerParams(vmem_limit_bytes=60 * 1024 * 1024),
        cost_estimate=COST,
    )(where, mine, twin_rows, halo)


def place_body(counts, where_ref, grid_ref, after_ref, *refs):
    parts, out_ref = refs[: len(counts)], refs[len(counts)]
    held, in_sems, out_sems = refs[len(counts) + 1 :]
    core = where_ref[0]
    ways = []
    for part, count in zip(parts, counts):
        for i in range(count):
            at = len(ways)
            column = pl.multiple_of((2 * where_ref[1 + at] + 1 - core) * QW, QW)
            ways.append(
                (
                    pltpu.make_async_copy(part.at[i], held.at[at], in_sems.at[at]),
                    pltpu.make_async_copy(
                        held.at[at], out_ref.at[:, pl.ds(column, QW)], out_sems.at[at]
                    ),
                )
            )
    for arrive, _ in ways:
        arrive.start()
    for arrive, leave in ways:
        arrive.wait()
        leave.start()
    for _, leave in ways:
        leave.wait()


def place(where, query_grad, parts, after):
    counts = tuple(part.shape[0] for part in parts)
    return pl.pallas_call(
        functools.partial(place_body, counts),
        grid_spec=pltpu.PrefetchScalarGridSpec(
            num_scalar_prefetch=1,
            grid=(),
            in_specs=[pl.BlockSpec(memory_space=pl.ANY)] * (2 + len(parts)),
            out_specs=pl.BlockSpec(memory_space=pl.ANY),
            scratch_shapes=[
                pltpu.VMEM((sum(counts), TOK, QW), jnp.bfloat16),
                pltpu.SemaphoreType.DMA((sum(counts),)),
                pltpu.SemaphoreType.DMA((sum(counts),)),
            ],
        ),
        out_shape=jax.ShapeDtypeStruct(query_grad.shape, query_grad.dtype),
        input_output_aliases={1: 0},
        cost_estimate=COST,
    )(where, query_grad, after, *parts)


NT = (((1,), (1,)), ((), ()))
NN = (((1,), (0,)), ((), ()))
TN = (((0,), (0,)), ((), ()))


def dot(a, b, dims):
    return lax.dot_general(a, b, dims, preferred_element_type=jnp.float32)


def attend_body(count, base, skipped, where_ref, *refs):
    latent_ref, rope_low_ref, rope_high_ref = refs[:3]
    q_ref, d_ref, twin_q_ref, twin_d_ref = refs[3:7]
    weights = refs[7 + skipped : 7 + skipped + 2 * count]
    at = 7 + skipped + 2 * count
    sums = refs[at : at + 2] if skipped else ()
    at += len(sums)
    query_out, twin_out, latent_out, rope_out, mark_out = refs[at : at + 5]
    wk_ref, wv_ref, q_both, d_both, grad_both, dk_ref, dv_ref = refs[at + 5 :]
    step = pl.program_id(0)
    core = where_ref[0]
    key_at = lax.broadcasted_iota(jnp.int32, (SPAN, TOK), 0)
    query_at = lax.broadcasted_iota(jnp.int32, (SPAN, TOK), 1)
    inside = (key_at > query_at) & (key_at <= query_at + WIN)
    started = key_at >= jnp.where(where_ref[CHIP_AT] > 0, 0, WIN)
    masks = (inside & started, inside)

    for i in range(count):

        @pl.when(step == i)
        def _():
            wk_ref[...] = weights[2 * i][...]
            wv_ref[...] = weights[2 * i + 1][...]

    for own in range(2):

        @pl.when(core == own)
        def _():
            q_both[own] = q_ref[...]
            d_both[own] = d_ref[...]
            q_both[1 - own] = twin_q_ref[...]
            d_both[1 - own] = twin_d_ref[...]

    latent = latent_ref[...]
    keys = dot(latent, wk_ref[...], NN)
    values = dot(latent, wv_ref[...], NN).astype(jnp.bfloat16)
    low = lax.broadcasted_iota(jnp.int32, (ROWS, NOPE), 1) < ROPE
    rope_sum = jnp.zeros((ROWS, NOPE), jnp.float32)

    def fold(first, second):
        return jnp.concatenate(
            [first[:TOK], first[TOK:] + second[:WIN], second[WIN:]], axis=0
        )

    for pair in range(GROUP // 2):
        query_parts = [[], []]
        key_parts = []
        for odd in range(2):
            head = 2 * pair + odd
            key = keys[:, head * NOPE : (head + 1) * NOPE]
            if odd:
                turned = pltpu.roll(key, ROPE, 1)
                tiles = [
                    jnp.where(low, 0.0, turned).astype(jnp.bfloat16),
                    jnp.where(low, turned, rope_high_ref[...]).astype(jnp.bfloat16),
                ]
            else:
                tiles = [key.astype(jnp.bfloat16), rope_low_ref[...]]
            wide = jnp.concatenate(tiles, axis=1)
            value = values[:, head * VDIM : (head + 1) * VDIM]
            start = pair * 2 * (NOPE + ROPE) + odd * NOPE
            dk, dv = [], []
            for s in range(2):
                span = slice(s * TOK, s * TOK + SPAN)
                q = q_both[s, :, start : start + 2 * NOPE]
                d = d_both[s, :, head * VDIM : (head + 1) * VDIM]
                scores = jnp.where(masks[s], dot(wide[span], q, NT) * SCALE, -jnp.inf)
                shifted = jnp.exp(scores - jnp.max(scores, axis=0, keepdims=True))
                inverse = 1.0 / jnp.sum(shifted, axis=0, keepdims=True)
                prob_grad = dot(value[span], d, NT)
                probs = shifted * inverse
                delta = jnp.sum(probs * prob_grad, axis=0, keepdims=True)
                score_grad = (SCALE * probs * (prob_grad - delta)).astype(jnp.bfloat16)
                probs_low = probs.astype(jnp.bfloat16)
                query_parts[s].append(dot(score_grad, wide[span], TN))
                dk.append(dot(score_grad, q, NN))
                dv.append(dot(probs_low, d, NN))
            dv_ref[:, head * VDIM : (head + 1) * VDIM] = fold(*dv).astype(jnp.bfloat16)
            key_parts.append(fold(*dk))
        even, odd = key_parts
        dk_ref[:, 2 * pair * NOPE : (2 * pair + 1) * NOPE] = even[:, :NOPE].astype(jnp.bfloat16)
        dk_ref[:, (2 * pair + 1) * NOPE : (2 * pair + 2) * NOPE] = pltpu.roll(
            jnp.where(low, odd[:, NOPE:], odd[:, :NOPE]), ROPE, 1
        ).astype(jnp.bfloat16)
        rope_sum = rope_sum + jnp.where(low, even[:, NOPE:], odd[:, NOPE:])
        for s in range(2):
            first, second = query_parts[s]
            left = pair * 3 * NOPE
            grad_both[s, :, left : left + NOPE] = first[:, :NOPE].astype(jnp.bfloat16)
            grad_both[s, :, left + NOPE : left + 2 * NOPE] = (
                first[:, NOPE:] + second[:, :NOPE]
            ).astype(jnp.bfloat16)
            grad_both[s, :, left + 2 * NOPE : left + 3 * NOPE] = second[:, NOPE:].astype(
                jnp.bfloat16
            )

    latent_sum = dot(dk_ref[...], wk_ref[...], NT) + dot(dv_ref[...], wv_ref[...], NT)

    @pl.when(step == 0)
    def _():
        latent_out[...] = sums[0][...] + latent_sum if sums else latent_sum
        rope_out[...] = sums[1][...] + rope_sum if sums else rope_sum
        mark_out[...] = jnp.zeros_like(mark_out)

    @pl.when(step > 0)
    def _():
        latent_out[...] += latent_sum
        rope_out[...] += rope_sum

    for own in range(2):

        @pl.when(core == own)
        def _():
            query_out[...] = grad_both[own]
            twin_out[0] = grad_both[1 - own]


def attend(
    where, base, shared, query, out_grad, twin_query, twin_grad, weights, earlier=(), after=(), heavy=1
):
    count = len(weights)
    skipped = list(earlier[:1]) + list(after)
    head_block = lambda width: pl.BlockSpec((TOK, width), lambda g, w: (0, 2 * w[base + g] + w[0]))
    whole = lambda shape: pl.BlockSpec(shape, lambda g, w: (0,) * len(shape))
    in_specs = [
        whole((ROWS, LATENT)),
        whole((ROWS, NOPE)),
        whole((ROWS, NOPE)),
        head_block(QW),
        head_block(VW),
        head_block(QW),
        head_block(VW),
    ]
    operands = [where, *shared, query, out_grad, twin_query, twin_grad, *skipped]
    in_specs += [pl.BlockSpec(memory_space=pl.ANY)] * len(skipped)
    for (key_part, key_at), (value_part, value_at) in weights:
        in_specs.append(pl.BlockSpec((LATENT, VW), lambda g, w, at=key_at: (at, 0)))
        in_specs.append(pl.BlockSpec((LATENT, VW), lambda g, w, at=value_at: (at, 0)))
        operands += [key_part, value_part]
    if earlier:
        in_specs += [whole((ROWS, LATENT)), whole((ROWS, NOPE))]
        operands += earlier[1:]
    query_grad, part, latent_sum, rope_sum, mark = pl.pallas_call(
        functools.partial(attend_body, count, base, len(skipped)),
        grid_spec=pltpu.PrefetchScalarGridSpec(
            num_scalar_prefetch=1,
            grid=(count,),
            in_specs=in_specs,
            out_specs=[
                head_block(QW),
                pl.BlockSpec((1, TOK, QW), lambda g, w: (g, 0, 0)),
                whole((ROWS, LATENT)),
                whole((ROWS, NOPE)),
                whole((8, NOPE)),
            ],
            scratch_shapes=[
                pltpu.VMEM((LATENT, VW), jnp.bfloat16),
                pltpu.VMEM((LATENT, VW), jnp.bfloat16),
                pltpu.VMEM((2, TOK, QW), jnp.bfloat16),
                pltpu.VMEM((2, TOK, VW), jnp.bfloat16),
                pltpu.VMEM((2, TOK, QW), jnp.bfloat16),
                pltpu.VMEM((ROWS, VW), jnp.bfloat16),
                pltpu.VMEM((ROWS, VW), jnp.bfloat16),
            ],
        ),
        out_shape=[
            jax.ShapeDtypeStruct((TOK, HEADS * (NOPE + ROPE)), jnp.bfloat16),
            jax.ShapeDtypeStruct((count, TOK, QW), jnp.bfloat16),
            jax.ShapeDtypeStruct((ROWS, LATENT), jnp.float32),
            jax.ShapeDtypeStruct((ROWS, NOPE), jnp.float32),
            jax.ShapeDtypeStruct((8, NOPE), jnp.float32),
        ],
        input_output_aliases={8: 0} if earlier else {},
        compiler_params=pltpu.CompilerParams(vmem_limit_bytes=60 * 1024 * 1024),
        cost_estimate=pl.CostEstimate(
            flops=heavy * count * 500_000_000, bytes_accessed=count * 500_000, transcendentals=0
        ),
    )(*operands)
    return query_grad, latent_sum, rope_sum, part, mark


def terms_body(where_ref, rows_ref, own_ref, other_ref, *refs):
    out_ref = refs[-1]
    here = where_ref[HALF_AT] * (EXP * CAP)
    there = (1 - where_ref[HALF_AT]) * (EXP * CAP)

    def rows(at):
        part = rows_ref[:, 0, pl.ds(pl.multiple_of(at, EXP * CAP), EXP * CAP), :]
        return part.reshape(4 * EXP * CAP, -1)

    total = dot(rows(here), own_ref[...], NN) + dot(rows(there), other_ref[...], NN)
    out_ref[...] = total.astype(jnp.bfloat16).reshape(out_ref.shape)


def terms(where, twin, slices, own_down, other_down, after):
    rows = slices.reshape(4, 2, 2 * EXP * CAP, -1)
    depth = rows.shape[3]
    weight = pl.BlockSpec((depth, FFH), lambda g, w: (0, 0))
    number = (lambda w: 1 - w[0]) if twin else (lambda w: w[0])
    return pl.pallas_call(
        terms_body,
        grid_spec=pltpu.PrefetchScalarGridSpec(
            num_scalar_prefetch=1,
            grid=(1,),
            in_specs=[
                pl.BlockSpec(
                    (4, 1, 2 * EXP * CAP, depth), lambda g, w: (0, number(w), 0, 0)
                ),
                weight,
                weight,
            ]
            + [pl.BlockSpec(memory_space=pl.ANY)] * len(after),
            out_specs=pl.BlockSpec((4, EXP * CAP, FFH), lambda g, w: (0, 0, 0)),
        ),
        out_shape=jax.ShapeDtypeStruct((4, EXP * CAP, FFH), jnp.bfloat16),
        compiler_params=pltpu.CompilerParams(vmem_limit_bytes=60 * 1024 * 1024),
        cost_estimate=pl.CostEstimate(
            flops=100_000_000, bytes_accessed=100_000, transcendentals=0
        ),
    )(where, rows, own_down, other_down, *after)


def local(
    query,
    out_grad,
    latent,
    rope_key,
    w_key,
    w_value,
    grad_stream,
    expert_ids,
    gate_weights,
    saved_hidden,
    w_down,
):
    query, out_grad, latent, rope_key = query[0], out_grad[0], latent[0], rope_key[0]
    grad_stream, expert_ids, gate_weights = grad_stream[0], expert_ids[0], gate_weights[0]
    index = lax.axis_index("ctx")
    core = index % 2
    chip = index // 2
    x = chip // 2
    half = chip % 2

    def group(step, flip):
        return 2 * ((x + step) % 4) + (half ^ flip)

    groups = [
        group(0, 0),
        group(-1, 0),
        group(1, 0),
        group(0, 1),
        group(2, 0),
        group(-1, 1),
        group(1, 1),
        group(2, 1),
    ]
    where = jnp.stack([core, *groups, chip, half]).astype(jnp.int32)

    def both(stack):
        return ((stack, 0), (stack, 1))

    mine = join(latent, rope_key.T)
    twin_rows = lax.ppermute(mine, "ctx", TWIN)
    halo = lax.ppermute(
        jnp.where(core == 0, twin_rows[TOK - WIN :], mine[TOK - WIN :]), "ctx", [(i, i + 2) for i in range(CTX - 2)]
    )
    own = stack(w_key, w_value)
    before = lax.ppermute(own, "ctx", RIGHT)
    after = lax.ppermute(own, "ctx", LEFT)
    beside = lax.ppermute(own, ("ctx", "exp"), ACROSS)
    twin_query = lax.ppermute(query, "ctx", TWIN)
    twin_grad = lax.ppermute(out_grad, "ctx", TWIN)
    down = w_down[0].T
    other_down = lax.ppermute(down, "ctx", [(i, i ^ 2) for i in range(CTX)])

    share = EXPERTS // EXP
    slots = jnp.arange(EXP * CAP, dtype=jnp.int32)[None, :]
    ids = tie(expert_ids, own)
    match = [ids[:, k : k + 1] == slots // CAP * share for k in range(TOPK)]
    live = functools.reduce(jnp.logical_or, match)
    token_at = jnp.arange(TOK, dtype=jnp.int32)
    earlier = dot(
        (token_at[:, None] > token_at[None, :]).astype(jnp.bfloat16), live.astype(jnp.bfloat16), NN
    )
    token_hot = (live & (earlier == (slots % CAP).astype(jnp.float32))).astype(jnp.bfloat16)
    gates = sum(
        jnp.where(match[k], gate_weights[:, k : k + 1].astype(jnp.float32), 0.0)
        for k in range(TOPK)
    )
    gate_send = jnp.sum(token_hot.astype(jnp.float32) * gates, axis=0).reshape(EXP, 1, CAP)
    outbound = dot(token_hot, grad_stream, TN).astype(jnp.bfloat16)
    tiles = outbound.shape[1] // NOPE
    outbound = jnp.concatenate(
        [
            outbound.reshape(EXP, CAP * tiles, NOPE),
            jnp.pad(gate_send.astype(jnp.bfloat16), ((0, 0), (0, 7), (0, NOPE - CAP))),
        ],
        axis=1,
    )
    outbound = tie(outbound, twin_query, own)
    routed = lax.all_to_all(outbound, "exp", split_axis=0, concat_axis=0, tiled=True)

    shared = prepare(where, mine, twin_rows, halo)
    common = (shared, query, out_grad, twin_query, twin_grad)

    *sums, part_a, mark_a = attend(where, 1, *common, [both(own)])

    opposite = lax.ppermute(before, "ctx", RIGHT)
    beside_after = lax.ppermute(beside, "ctx", LEFT)
    beside_before = lax.ppermute(before, ("ctx", "exp"), ACROSS)
    *sums, part_b, mark_b = attend(
        where, 2, *common, [both(before), both(after)], sums, heavy=10
    )
    routed = tie(routed, mark_b, other_down)
    row_gate = routed[:, CAP * tiles, :CAP].reshape(EXP * CAP, 1)
    slices = routed[:, : CAP * tiles].reshape(EXP * CAP, 4, 2, 2, -1)
    slices = slices.transpose(1, 3, 2, 0, 4).reshape(CHIPS, 2 * EXP * CAP, -1)
    sent = slices
    slices = lax.all_to_all(
        slices, "ctx", split_axis=0, concat_axis=0, tiled=True, axis_index_groups=RING
    )

    *sums, part_d, mark_d = attend(where, 4, *common, [both(beside)], sums, (sent,))
    part_a = lax.ppermute(part_a, "ctx", TWIN)
    part_d = lax.ppermute(part_d, "ctx", TWIN)
    part_b = lax.ppermute(part_b, "ctx", TWIN)

    beside_after = tie(beside_after, mark_d)
    opposite = tie(opposite, mark_d)
    key_half = beside_after[:LATENT]
    value_half = opposite[LATENT:]
    last_key = lax.ppermute(key_half, "ctx", LEFT)
    last_value = lax.ppermute(value_half, ("ctx", "exp"), ACROSS)

    give = terms(
        where, True, slices, down, other_down, (mark_b, beside_before, key_half, value_half)
    )
    keep = terms(where, False, slices, down, other_down, (give,))
    taken = lax.ppermute(give, "ctx", TWIN)

    keep = (keep.astype(jnp.float32) + taken.astype(jnp.float32)).astype(jnp.bfloat16)
    pieces = lax.all_to_all(
        keep, "ctx", split_axis=0, concat_axis=0, tiled=True, axis_index_groups=RING_CORE
    )

    *sums, part_c, mark_c = attend(
        where,
        5,
        *common,
        [
            both(opposite),
            both(beside_before),
            both(beside_after),
            ((last_key, 0), (last_value, 0)),
        ],
        sums,
        (keep,),
    )
    part_c = lax.ppermute(part_c, "ctx", TWIN)

    query_grad, latent_sum, rope_sum = sums
    latent_sum = tie(latent_sum, pieces)
    sums = jnp.concatenate([latent_sum, rope_sum[:, :ROPE] + rope_sum[:, ROPE:]], axis=1)
    back = lax.ppermute(sums[:WIN], "ctx", [(i + 2, i) for i in range(CTX - 2)])
    low = sums[WIN : WIN + TOK]
    high = sums[WIN + TOK :]
    high = jnp.concatenate([high[: TOK - WIN], high[TOK - WIN :] + back], axis=0)
    kept = jnp.where(core == 0, low, high)
    given = lax.ppermute(jnp.where(core == 0, high, low), "ctx", TWIN)
    total = (kept + given).astype(jnp.bfloat16)
    raw_grad = jnp.sum(pieces.astype(jnp.float32), axis=0)
    gate_part = jnp.sum(saved_hidden[0, 0].astype(jnp.float32) * raw_grad, axis=1)
    hidden_grad = (row_gate.astype(jnp.float32) * raw_grad).astype(jnp.bfloat16)
    returned = lax.all_to_all(
        gate_part.reshape(EXP, CAP), "exp", split_axis=0, concat_axis=0, tiled=True
    )
    query_grad = place(where, query_grad, (part_a, part_b, part_d, part_c), gate_part[None])
    found = token_hot.astype(jnp.float32) * returned.reshape(1, -1)
    gate_grad = jnp.stack(
        [jnp.sum(jnp.where(match[k], found, 0.0), axis=1) for k in range(TOPK)], axis=1
    )
    return (
        query_grad[None],
        total[None, :, :LATENT],
        total[None, :, LATENT:],
        hidden_grad[None, None],
        gate_grad[None],
    )


def solution(mesh):
    in_specs = (
        P("exp", "ctx", None),
        P("exp", "ctx", None),
        P("exp", "ctx", None),
        P("exp", "ctx", None),
        P(None, "ctx"),
        P(None, "ctx"),
        P("exp", "ctx", None),
        P("exp", "ctx", None),
        P("exp", "ctx", None),
        P("ctx", "exp", None, None),
        P("exp", None, "ctx"),
    )
    out_specs = (
        P("exp", "ctx", None),
        P("exp", "ctx", None),
        P("exp", "ctx", None),
        P("ctx", "exp", None, None),
        P("exp", "ctx", None),
    )
    return jax.shard_map(local, mesh=mesh, in_specs=in_specs, out_specs=out_specs, check_vma=False)
```

```python
import functools

import jax
import jax.numpy as jnp
from jax import lax
from jax.experimental import pallas as pl
from jax.experimental.pallas import tpu as pltpu
from jax.sharding import PartitionSpec as P

HEADS = 64
NOPE = 128
ROPE = 64
VDIM = 128
LATENT = 512
FFH = 1536
EXPERTS = 160
TOPK = 6
WIN = 32
CAP = 6
CTX = 16
EXP = 16
TOK = 128
CHIPS = 8
GROUP = 4
QW = GROUP * (NOPE + ROPE)
VW = GROUP * VDIM
ROWS = 2 * TOK + WIN
SPAN = TOK + WIN
SCALE = (NOPE + ROPE) ** (-0.5)
CHIP_AT, HALF_AT = 9, 10
COST = pl.CostEstimate(flops=1_000_000, bytes_accessed=1_000_000, transcendentals=0)


def ctx_at(x, half, core):
    return ((x % 4) * 2 + half) * 2 + core


def ctx_moves(step):
    return [
        (ctx_at(x, half, core), ctx_at(x + step, half, core))
        for x in range(4)
        for half in range(2)
        for core in range(2)
    ]


RIGHT = ctx_moves(1)
LEFT = ctx_moves(-1)
TWIN = [(i, i ^ 1) for i in range(CTX)]
ACROSS = [
    ((i * EXP + e), ((i ^ 2) * EXP + (e ^ 8))) for i in range(CTX) for e in range(EXP)
]
RING = [[ctx_at(x, half, core) for x in range(4) for core in range(2)] for half in range(2)]
RING_CORE = [[ctx_at(x, half, core) for x in range(4)] for half in range(2) for core in range(2)]


def nothing_body(*refs):
    pass


def tie(value, *others):
    return pl.pallas_call(
        nothing_body,
        in_specs=[pl.BlockSpec(memory_space=pl.ANY)] * (1 + len(others)),
        out_specs=pl.BlockSpec(memory_space=pl.ANY),
        out_shape=jax.ShapeDtypeStruct(value.shape, value.dtype),
        input_output_aliases={0: 0},
        cost_estimate=COST,
    )(value, *others)


def stack_body(key_ref, value_ref, out_ref):
    out_ref[:LATENT] = key_ref[...]
    out_ref[LATENT:] = value_ref[...]


def stack(w_key, w_value):
    return pl.pallas_call(
        stack_body,
        out_shape=jax.ShapeDtypeStruct((2 * LATENT, VW), jnp.bfloat16),
        compiler_params=pltpu.CompilerParams(vmem_limit_bytes=60 * 1024 * 1024),
        cost_estimate=COST,
    )(w_key, w_value)


def join_body(latent_ref, rope_ref, out_ref):
    out_ref[:, :LATENT] = latent_ref[...]
    rope = rope_ref[...].astype(jnp.float32).T
    out_ref[:, LATENT:] = jnp.concatenate([rope, jnp.zeros_like(rope)], axis=1).astype(jnp.bfloat16)


def join(latent, rope_turned):
    return pl.pallas_call(
        join_body,
        out_shape=jax.ShapeDtypeStruct((TOK, LATENT + NOPE), jnp.bfloat16),
        compiler_params=pltpu.CompilerParams(vmem_limit_bytes=60 * 1024 * 1024),
        cost_estimate=COST,
    )(latent, rope_turned)


def prepare_body(where_ref, mine_ref, twin_ref, halo_ref, latent_ref, low_ref, high_ref):
    core = where_ref[0]

    def put(at, ref):
        rows = pl.ds(at, ref.shape[0])
        latent_ref[rows, :] = ref[:, :LATENT]
        rope = ref[:, LATENT:]
        low_ref[rows, :] = rope
        high_ref[rows, :] = pltpu.roll(rope.astype(jnp.float32), ROPE, 1)

    put(0, halo_ref)
    for own in range(2):

        @pl.when(core == own)
        def _():
            put(WIN + own * TOK, mine_ref)
            put(WIN + (1 - own) * TOK, twin_ref)


def prepare(where, mine, twin_rows, halo):
    return pl.pallas_call(
        prepare_body,
        in_specs=[pl.BlockSpec(memory_space=pltpu.SMEM)]
        + [pl.BlockSpec(memory_space=pltpu.VMEM)] * 3,
        out_shape=[
            jax.ShapeDtypeStruct((ROWS, LATENT), jnp.bfloat16),
            jax.ShapeDtypeStruct((ROWS, NOPE), jnp.bfloat16),
            jax.ShapeDtypeStruct((ROWS, NOPE), jnp.float32),
        ],
        compiler_params=pltpu.CompilerParams(vmem_limit_bytes=60 * 1024 * 1024),
        cost_estimate=COST,
    )(where, mine, twin_rows, halo)


def place_body(counts, where_ref, grid_ref, after_ref, *refs):
    parts, out_ref = refs[: len(counts)], refs[len(counts)]
    held, in_sems, out_sems = refs[len(counts) + 1 :]
    core = where_ref[0]
    ways = []
    for part, count in zip(parts, counts):
        for i in range(count):
            at = len(ways)
            column = pl.multiple_of((2 * where_ref[1 + at] + 1 - core) * QW, QW)
            ways.append(
                (
                    pltpu.make_async_copy(part.at[i], held.at[at], in_sems.at[at]),
                    pltpu.make_async_copy(
                        held.at[at], out_ref.at[:, pl.ds(column, QW)], out_sems.at[at]
                    ),
                )
            )
    for arrive, _ in ways:
        arrive.start()
    for arrive, leave in ways:
        arrive.wait()
        leave.start()
    for _, leave in ways:
        leave.wait()


def place(where, query_grad, parts, after):
    counts = tuple(part.shape[0] for part in parts)
    return pl.pallas_call(
        functools.partial(place_body, counts),
        grid_spec=pltpu.PrefetchScalarGridSpec(
            num_scalar_prefetch=1,
            grid=(),
            in_specs=[pl.BlockSpec(memory_space=pl.ANY)] * (2 + len(parts)),
            out_specs=pl.BlockSpec(memory_space=pl.ANY),
            scratch_shapes=[
                pltpu.VMEM((sum(counts), TOK, QW), jnp.bfloat16),
                pltpu.SemaphoreType.DMA((sum(counts),)),
                pltpu.SemaphoreType.DMA((sum(counts),)),
            ],
        ),
        out_shape=jax.ShapeDtypeStruct(query_grad.shape, query_grad.dtype),
        input_output_aliases={1: 0},
        cost_estimate=COST,
    )(where, query_grad, after, *parts)


NT = (((1,), (1,)), ((), ()))
NN = (((1,), (0,)), ((), ()))
TN = (((0,), (0,)), ((), ()))


def dot(a, b, dims):
    return lax.dot_general(a, b, dims, preferred_element_type=jnp.float32)


def attend_body(count, base, skipped, where_ref, *refs):
    latent_ref, rope_low_ref, rope_high_ref = refs[:3]
    q_ref, d_ref, twin_q_ref, twin_d_ref = refs[3:7]
    weights = refs[7 + skipped : 7 + skipped + 2 * count]
    at = 7 + skipped + 2 * count
    sums = refs[at : at + 2] if skipped else ()
    at += len(sums)
    query_out, twin_out, latent_out, rope_out, mark_out = refs[at : at + 5]
    wk_ref, wv_ref, q_both, d_both, grad_both, dk_ref, dv_ref = refs[at + 5 :]
    step = pl.program_id(0)
    core = where_ref[0]
    key_at = lax.broadcasted_iota(jnp.int32, (SPAN, TOK), 0)
    query_at = lax.broadcasted_iota(jnp.int32, (SPAN, TOK), 1)
    inside = (key_at > query_at) & (key_at <= query_at + WIN)
    started = key_at >= jnp.where(where_ref[CHIP_AT] > 0, 0, WIN)
    masks = (inside & started, inside)

    for i in range(count):

        @pl.when(step == i)
        def _():
            wk_ref[...] = weights[2 * i][...]
            wv_ref[...] = weights[2 * i + 1][...]

    for own in range(2):

        @pl.when(core == own)
        def _():
            q_both[own] = q_ref[...]
            d_both[own] = d_ref[...]
            q_both[1 - own] = twin_q_ref[...]
            d_both[1 - own] = twin_d_ref[...]

    latent = latent_ref[...]
    keys = dot(latent, wk_ref[...], NN)
    values = dot(latent, wv_ref[...], NN).astype(jnp.bfloat16)
    low = lax.broadcasted_iota(jnp.int32, (ROWS, NOPE), 1) < ROPE
    rope_sum = jnp.zeros((ROWS, NOPE), jnp.float32)

    def fold(first, second):
        return jnp.concatenate(
            [first[:TOK], first[TOK:] + second[:WIN], second[WIN:]], axis=0
        )

    for pair in range(GROUP // 2):
        query_parts = [[], []]
        key_parts = []
        for odd in range(2):
            head = 2 * pair + odd
            key = keys[:, head * NOPE : (head + 1) * NOPE]
            if odd:
                turned = pltpu.roll(key, ROPE, 1)
                tiles = [
                    jnp.where(low, 0.0, turned).astype(jnp.bfloat16),
                    jnp.where(low, turned, rope_high_ref[...]).astype(jnp.bfloat16),
                ]
            else:
                tiles = [key.astype(jnp.bfloat16), rope_low_ref[...]]
            wide = jnp.concatenate(tiles, axis=1)
            value = values[:, head * VDIM : (head + 1) * VDIM]
            start = pair * 2 * (NOPE + ROPE) + odd * NOPE
            dk, dv = [], []
            for s in range(2):
                span = slice(s * TOK, s * TOK + SPAN)
                q = q_both[s, :, start : start + 2 * NOPE]
                d = d_both[s, :, head * VDIM : (head + 1) * VDIM]
                scores = jnp.where(masks[s], dot(wide[span], q, NT) * SCALE, -jnp.inf)
                shifted = jnp.exp(scores - jnp.max(scores, axis=0, keepdims=True))
                inverse = 1.0 / jnp.sum(shifted, axis=0, keepdims=True)
                prob_grad = dot(value[span], d, NT)
                probs = shifted * inverse
                delta = jnp.sum(probs * prob_grad, axis=0, keepdims=True)
                score_grad = (SCALE * probs * (prob_grad - delta)).astype(jnp.bfloat16)
                probs_low = probs.astype(jnp.bfloat16)
                query_parts[s].append(dot(score_grad, wide[span], TN))
                dk.append(dot(score_grad, q, NN))
                dv.append(dot(probs_low, d, NN))
            dv_ref[:, head * VDIM : (head + 1) * VDIM] = fold(*dv).astype(jnp.bfloat16)
            key_parts.append(fold(*dk))
        even, odd = key_parts
        dk_ref[:, 2 * pair * NOPE : (2 * pair + 1) * NOPE] = even[:, :NOPE].astype(jnp.bfloat16)
        dk_ref[:, (2 * pair + 1) * NOPE : (2 * pair + 2) * NOPE] = pltpu.roll(
            jnp.where(low, odd[:, NOPE:], odd[:, :NOPE]), ROPE, 1
        ).astype(jnp.bfloat16)
        rope_sum = rope_sum + jnp.where(low, even[:, NOPE:], odd[:, NOPE:])
        for s in range(2):
            first, second = query_parts[s]
            left = pair * 3 * NOPE
            grad_both[s, :, left : left + NOPE] = first[:, :NOPE].astype(jnp.bfloat16)
            grad_both[s, :, left + NOPE : left + 2 * NOPE] = (
                first[:, NOPE:] + second[:, :NOPE]
            ).astype(jnp.bfloat16)
            grad_both[s, :, left + 2 * NOPE : left + 3 * NOPE] = second[:, NOPE:].astype(
                jnp.bfloat16
            )

    latent_sum = dot(dk_ref[...], wk_ref[...], NT) + dot(dv_ref[...], wv_ref[...], NT)

    @pl.when(step == 0)
    def _():
        latent_out[...] = sums[0][...] + latent_sum if sums else latent_sum
        rope_out[...] = sums[1][...] + rope_sum if sums else rope_sum
        mark_out[...] = jnp.zeros_like(mark_out)

    @pl.when(step > 0)
    def _():
        latent_out[...] += latent_sum
        rope_out[...] += rope_sum

    for own in range(2):

        @pl.when(core == own)
        def _():
            query_out[...] = grad_both[own]
            twin_out[0] = grad_both[1 - own]


def attend(
    where, base, shared, query, out_grad, twin_query, twin_grad, weights, earlier=(), after=(), heavy=1
):
    count = len(weights)
    skipped = list(earlier[:1]) + list(after)
    head_block = lambda width: pl.BlockSpec((TOK, width), lambda g, w: (0, 2 * w[base + g] + w[0]))
    whole = lambda shape: pl.BlockSpec(shape, lambda g, w: (0,) * len(shape))
    in_specs = [
        whole((ROWS, LATENT)),
        whole((ROWS, NOPE)),
        whole((ROWS, NOPE)),
        head_block(QW),
        head_block(VW),
        head_block(QW),
        head_block(VW),
    ]
    operands = [where, *shared, query, out_grad, twin_query, twin_grad, *skipped]
    in_specs += [pl.BlockSpec(memory_space=pl.ANY)] * len(skipped)
    for (key_part, key_at), (value_part, value_at) in weights:
        in_specs.append(pl.BlockSpec((LATENT, VW), lambda g, w, at=key_at: (at, 0)))
        in_specs.append(pl.BlockSpec((LATENT, VW), lambda g, w, at=value_at: (at, 0)))
        operands += [key_part, value_part]
    if earlier:
        in_specs += [whole((ROWS, LATENT)), whole((ROWS, NOPE))]
        operands += earlier[1:]
    query_grad, part, latent_sum, rope_sum, mark = pl.pallas_call(
        functools.partial(attend_body, count, base, len(skipped)),
        grid_spec=pltpu.PrefetchScalarGridSpec(
            num_scalar_prefetch=1,
            grid=(count,),
            in_specs=in_specs,
            out_specs=[
                head_block(QW),
                pl.BlockSpec((1, TOK, QW), lambda g, w: (g, 0, 0)),
                whole((ROWS, LATENT)),
                whole((ROWS, NOPE)),
                whole((8, NOPE)),
            ],
            scratch_shapes=[
                pltpu.VMEM((LATENT, VW), jnp.bfloat16),
                pltpu.VMEM((LATENT, VW), jnp.bfloat16),
                pltpu.VMEM((2, TOK, QW), jnp.bfloat16),
                pltpu.VMEM((2, TOK, VW), jnp.bfloat16),
                pltpu.VMEM((2, TOK, QW), jnp.bfloat16),
                pltpu.VMEM((ROWS, VW), jnp.bfloat16),
                pltpu.VMEM((ROWS, VW), jnp.bfloat16),
            ],
        ),
        out_shape=[
            jax.ShapeDtypeStruct((TOK, HEADS * (NOPE + ROPE)), jnp.bfloat16),
            jax.ShapeDtypeStruct((count, TOK, QW), jnp.bfloat16),
            jax.ShapeDtypeStruct((ROWS, LATENT), jnp.float32),
            jax.ShapeDtypeStruct((ROWS, NOPE), jnp.float32),
            jax.ShapeDtypeStruct((8, NOPE), jnp.float32),
        ],
        input_output_aliases={8: 0} if earlier else {},
        compiler_params=pltpu.CompilerParams(vmem_limit_bytes=60 * 1024 * 1024),
        cost_estimate=pl.CostEstimate(
            flops=heavy * count * 500_000_000, bytes_accessed=count * 500_000, transcendentals=0
        ),
    )(*operands)
    return query_grad, latent_sum, rope_sum, part, mark


def terms_body(where_ref, rows_ref, own_ref, other_ref, *refs):
    out_ref = refs[-1]
    here = where_ref[HALF_AT] * (EXP * CAP)
    there = (1 - where_ref[HALF_AT]) * (EXP * CAP)

    def rows(at):
        part = rows_ref[:, 0, pl.ds(pl.multiple_of(at, EXP * CAP), EXP * CAP), :]
        return part.reshape(4 * EXP * CAP, -1)

    total = dot(rows(here), own_ref[...], NN) + dot(rows(there), other_ref[...], NN)
    out_ref[...] = total.astype(jnp.bfloat16).reshape(out_ref.shape)


def terms(where, twin, slices, own_down, other_down, after):
    rows = slices.reshape(4, 2, 2 * EXP * CAP, -1)
    depth = rows.shape[3]
    weight = pl.BlockSpec((depth, FFH), lambda g, w: (0, 0))
    number = (lambda w: 1 - w[0]) if twin else (lambda w: w[0])
    return pl.pallas_call(
        terms_body,
        grid_spec=pltpu.PrefetchScalarGridSpec(
            num_scalar_prefetch=1,
            grid=(1,),
            in_specs=[
                pl.BlockSpec(
                    (4, 1, 2 * EXP * CAP, depth), lambda g, w: (0, number(w), 0, 0)
                ),
                weight,
                weight,
            ]
            + [pl.BlockSpec(memory_space=pl.ANY)] * len(after),
            out_specs=pl.BlockSpec((4, EXP * CAP, FFH), lambda g, w: (0, 0, 0)),
        ),
        out_shape=jax.ShapeDtypeStruct((4, EXP * CAP, FFH), jnp.bfloat16),
        compiler_params=pltpu.CompilerParams(vmem_limit_bytes=60 * 1024 * 1024),
        cost_estimate=pl.CostEstimate(
            flops=100_000_000, bytes_accessed=100_000, transcendentals=0
        ),
    )(where, rows, own_down, other_down, *after)


def local(
    query,
    out_grad,
    latent,
    rope_key,
    w_key,
    w_value,
    grad_stream,
    expert_ids,
    gate_weights,
    saved_hidden,
    w_down,
):
    query, out_grad, latent, rope_key = query[0], out_grad[0], latent[0], rope_key[0]
    grad_stream, expert_ids, gate_weights = grad_stream[0], expert_ids[0], gate_weights[0]
    index = lax.axis_index("ctx")
    core = index % 2
    chip = index // 2
    x = chip // 2
    half = chip % 2

    def group(step, flip):
        return 2 * ((x + step) % 4) + (half ^ flip)

    groups = [
        group(0, 0),
        group(-1, 0),
        group(1, 0),
        group(0, 1),
        group(2, 0),
        group(-1, 1),
        group(1, 1),
        group(2, 1),
    ]
    where = jnp.stack([core, *groups, chip, half]).astype(jnp.int32)

    def both(stack):
        return ((stack, 0), (stack, 1))

    mine = join(latent, rope_key.T)
    twin_rows = lax.ppermute(mine, "ctx", TWIN)
    halo = lax.ppermute(
        jnp.where(core == 0, twin_rows[TOK - WIN :], mine[TOK - WIN :]), "ctx", [(i, i + 2) for i in range(CTX - 2)]
    )
    own = stack(w_key, w_value)
    before = lax.ppermute(own, "ctx", RIGHT)
    after = lax.ppermute(own, "ctx", LEFT)
    beside = lax.ppermute(own, ("ctx", "exp"), ACROSS)
    twin_query = lax.ppermute(query, "ctx", TWIN)
    twin_grad = lax.ppermute(out_grad, "ctx", TWIN)
    down = w_down[0].T
    other_down = lax.ppermute(down, "ctx", [(i, i ^ 2) for i in range(CTX)])

    share = EXPERTS // EXP
    slots = jnp.arange(EXP * CAP, dtype=jnp.int32)[None, :]
    ids = tie(expert_ids, own)
    match = [ids[:, k : k + 1] == slots // CAP * share for k in range(TOPK)]
    live = functools.reduce(jnp.logical_or, match)
    token_at = jnp.arange(TOK, dtype=jnp.int32)
    earlier = dot(
        (token_at[:, None] > token_at[None, :]).astype(jnp.bfloat16), live.astype(jnp.bfloat16), NN
    )
    token_hot = (live & (earlier == (slots % CAP).astype(jnp.float32))).astype(jnp.bfloat16)
    gates = sum(
        jnp.where(match[k], gate_weights[:, k : k + 1].astype(jnp.float32), 0.0)
        for k in range(TOPK)
    )
    gate_send = jnp.sum(token_hot.astype(jnp.float32) * gates, axis=0).reshape(EXP, 1, CAP)
    outbound = dot(token_hot, grad_stream, TN).astype(jnp.bfloat16)
    tiles = outbound.shape[1] // NOPE
    outbound = jnp.concatenate(
        [
            outbound.reshape(EXP, CAP * tiles, NOPE),
            jnp.pad(gate_send.astype(jnp.bfloat16), ((0, 0), (0, 7), (0, NOPE - CAP))),
        ],
        axis=1,
    )
    outbound = tie(outbound, twin_query, own)
    routed = lax.all_to_all(outbound, "exp", split_axis=0, concat_axis=0, tiled=True)

    shared = prepare(where, mine, twin_rows, halo)
    common = (shared, query, out_grad, twin_query, twin_grad)

    *sums, part_a, mark_a = attend(where, 1, *common, [both(own)])

    opposite = lax.ppermute(before, "ctx", RIGHT)
    beside_after = lax.ppermute(beside, "ctx", LEFT)
    beside_before = lax.ppermute(before, ("ctx", "exp"), ACROSS)
    *sums, part_b, mark_b = attend(
        where, 2, *common, [both(before), both(after)], sums, heavy=10
    )
    routed = tie(routed, mark_b, other_down)
    row_gate = routed[:, CAP * tiles, :CAP].reshape(EXP * CAP, 1)
    slices = routed[:, : CAP * tiles].reshape(EXP * CAP, 4, 2, 2, -1)
    slices = slices.transpose(1, 3, 2, 0, 4).reshape(CHIPS, 2 * EXP * CAP, -1)
    sent = slices
    slices = lax.all_to_all(
        slices, "ctx", split_axis=0, concat_axis=0, tiled=True, axis_index_groups=RING
    )

    *sums, part_d, mark_d = attend(
        where, 4, *common, [both(beside), both(opposite)], sums, (sent,)
    )
    part_a = lax.ppermute(part_a, "ctx", TWIN)
    part_d = lax.ppermute(part_d, "ctx", TWIN)
    part_b = lax.ppermute(part_b, "ctx", TWIN)

    beside_after = tie(beside_after, mark_d)
    key_half = beside_after[:LATENT]
    value_half = tie(opposite[LATENT:], mark_d)
    last_key = lax.ppermute(key_half, "ctx", LEFT)
    last_value = lax.ppermute(value_half, ("ctx", "exp"), ACROSS)

    give = terms(
        where, True, slices, down, other_down, (mark_b, beside_before, key_half, value_half)
    )
    keep = terms(where, False, slices, down, other_down, (give,))
    taken = lax.ppermute(give, "ctx", TWIN)

    keep = (keep.astype(jnp.float32) + taken.astype(jnp.float32)).astype(jnp.bfloat16)
    pieces = lax.all_to_all(
        keep, "ctx", split_axis=0, concat_axis=0, tiled=True, axis_index_groups=RING_CORE
    )

    *sums, part_c, mark_c = attend(
        where,
        6,
        *common,
        [
            both(beside_before),
            both(beside_after),
            ((last_key, 0), (last_value, 0)),
        ],
        sums,
        (keep,),
    )
    part_c = lax.ppermute(part_c, "ctx", TWIN)

    query_grad, latent_sum, rope_sum = sums
    latent_sum = tie(latent_sum, pieces)
    sums = jnp.concatenate([latent_sum, rope_sum[:, :ROPE] + rope_sum[:, ROPE:]], axis=1)
    back = lax.ppermute(sums[:WIN], "ctx", [(i + 2, i) for i in range(CTX - 2)])
    low = sums[WIN : WIN + TOK]
    high = sums[WIN + TOK :]
    high = jnp.concatenate([high[: TOK - WIN], high[TOK - WIN :] + back], axis=0)
    kept = jnp.where(core == 0, low, high)
    given = lax.ppermute(jnp.where(core == 0, high, low), "ctx", TWIN)
    total = (kept + given).astype(jnp.bfloat16)
    raw_grad = jnp.sum(pieces.astype(jnp.float32), axis=0)
    gate_part = jnp.sum(saved_hidden[0, 0].astype(jnp.float32) * raw_grad, axis=1)
    hidden_grad = (row_gate.astype(jnp.float32) * raw_grad).astype(jnp.bfloat16)
    returned = lax.all_to_all(
        gate_part.reshape(EXP, CAP), "exp", split_axis=0, concat_axis=0, tiled=True
    )
    query_grad = place(where, query_grad, (part_a, part_b, part_d, part_c), gate_part[None])
    found = token_hot.astype(jnp.float32) * returned.reshape(1, -1)
    gate_grad = jnp.stack(
        [jnp.sum(jnp.where(match[k], found, 0.0), axis=1) for k in range(TOPK)], axis=1
    )
    return (
        query_grad[None],
        total[None, :, :LATENT],
        total[None, :, LATENT:],
        hidden_grad[None, None],
        gate_grad[None],
    )


def solution(mesh):
    in_specs = (
        P("exp", "ctx", None),
        P("exp", "ctx", None),
        P("exp", "ctx", None),
        P("exp", "ctx", None),
        P(None, "ctx"),
        P(None, "ctx"),
        P("exp", "ctx", None),
        P("exp", "ctx", None),
        P("exp", "ctx", None),
        P("ctx", "exp", None, None),
        P("exp", None, "ctx"),
    )
    out_specs = (
        P("exp", "ctx", None),
        P("exp", "ctx", None),
        P("exp", "ctx", None),
        P("ctx", "exp", None, None),
        P("exp", "ctx", None),
    )
    return jax.shard_map(local, mesh=mesh, in_specs=in_specs, out_specs=out_specs, check_vma=False)
```

```python
import functools

import jax
import jax.numpy as jnp
from jax import lax
from jax.experimental import pallas as pl
from jax.experimental.pallas import tpu as pltpu
from jax.sharding import PartitionSpec as P

HEADS = 64
NOPE = 128
ROPE = 64
VDIM = 128
LATENT = 512
FFH = 1536
EXPERTS = 160
TOPK = 6
WIN = 32
CAP = 6
CTX = 16
EXP = 16
TOK = 128
CHIPS = 8
GROUP = 4
QW = GROUP * (NOPE + ROPE)
VW = GROUP * VDIM
ROWS = 2 * TOK + WIN
SPAN = TOK + WIN
SCALE = (NOPE + ROPE) ** (-0.5)
CHIP_AT, HALF_AT = 9, 10
COST = pl.CostEstimate(flops=1_000_000, bytes_accessed=1_000_000, transcendentals=0)


def ctx_at(x, half, core):
    return ((x % 4) * 2 + half) * 2 + core


def ctx_moves(step):
    return [
        (ctx_at(x, half, core), ctx_at(x + step, half, core))
        for x in range(4)
        for half in range(2)
        for core in range(2)
    ]


RIGHT = ctx_moves(1)
LEFT = ctx_moves(-1)
TWIN = [(i, i ^ 1) for i in range(CTX)]
ACROSS = [
    ((i * EXP + e), ((i ^ 2) * EXP + (e ^ 8))) for i in range(CTX) for e in range(EXP)
]
RING = [[ctx_at(x, half, core) for x in range(4) for core in range(2)] for half in range(2)]
RING_CORE = [[ctx_at(x, half, core) for x in range(4)] for half in range(2) for core in range(2)]


def nothing_body(*refs):
    pass


def tie(value, *others):
    return pl.pallas_call(
        nothing_body,
        in_specs=[pl.BlockSpec(memory_space=pl.ANY)] * (1 + len(others)),
        out_specs=pl.BlockSpec(memory_space=pl.ANY),
        out_shape=jax.ShapeDtypeStruct(value.shape, value.dtype),
        input_output_aliases={0: 0},
        cost_estimate=COST,
    )(value, *others)


def stack_body(key_ref, value_ref, out_ref):
    out_ref[:LATENT] = key_ref[...]
    out_ref[LATENT:] = value_ref[...]


def stack(w_key, w_value):
    return pl.pallas_call(
        stack_body,
        out_shape=jax.ShapeDtypeStruct((2 * LATENT, VW), jnp.bfloat16),
        compiler_params=pltpu.CompilerParams(vmem_limit_bytes=60 * 1024 * 1024),
        cost_estimate=COST,
    )(w_key, w_value)


def join_body(latent_ref, rope_ref, out_ref):
    out_ref[:, :LATENT] = latent_ref[...]
    rope = rope_ref[...].astype(jnp.float32).T
    out_ref[:, LATENT:] = jnp.concatenate([rope, jnp.zeros_like(rope)], axis=1).astype(jnp.bfloat16)


def join(latent, rope_turned):
    return pl.pallas_call(
        join_body,
        out_shape=jax.ShapeDtypeStruct((TOK, LATENT + NOPE), jnp.bfloat16),
        compiler_params=pltpu.CompilerParams(vmem_limit_bytes=60 * 1024 * 1024),
        cost_estimate=COST,
    )(latent, rope_turned)


def prepare_body(where_ref, mine_ref, twin_ref, halo_ref, latent_ref, low_ref, high_ref):
    core = where_ref[0]

    def put(at, ref):
        rows = pl.ds(at, ref.shape[0])
        latent_ref[rows, :] = ref[:, :LATENT]
        rope = ref[:, LATENT:]
        low_ref[rows, :] = rope
        high_ref[rows, :] = pltpu.roll(rope.astype(jnp.float32), ROPE, 1)

    put(0, halo_ref)
    for own in range(2):

        @pl.when(core == own)
        def _():
            put(WIN + own * TOK, mine_ref)
            put(WIN + (1 - own) * TOK, twin_ref)


def prepare(where, mine, twin_rows, halo):
    return pl.pallas_call(
        prepare_body,
        in_specs=[pl.BlockSpec(memory_space=pltpu.SMEM)]
        + [pl.BlockSpec(memory_space=pltpu.VMEM)] * 3,
        out_shape=[
            jax.ShapeDtypeStruct((ROWS, LATENT), jnp.bfloat16),
            jax.ShapeDtypeStruct((ROWS, NOPE), jnp.bfloat16),
            jax.ShapeDtypeStruct((ROWS, NOPE), jnp.float32),
        ],
        compiler_params=pltpu.CompilerParams(vmem_limit_bytes=60 * 1024 * 1024),
        cost_estimate=COST,
    )(where, mine, twin_rows, halo)


def place_body(counts, where_ref, grid_ref, after_ref, *refs):
    parts, out_ref = refs[: len(counts)], refs[len(counts)]
    held, in_sems, out_sems = refs[len(counts) + 1 :]
    core = where_ref[0]
    ways = []
    for part, count in zip(parts, counts):
        for i in range(count):
            at = len(ways)
            column = pl.multiple_of((2 * where_ref[1 + at] + 1 - core) * QW, QW)
            ways.append(
                (
                    pltpu.make_async_copy(part.at[i], held.at[at], in_sems.at[at]),
                    pltpu.make_async_copy(
                        held.at[at], out_ref.at[:, pl.ds(column, QW)], out_sems.at[at]
                    ),
                )
            )
    for arrive, _ in ways:
        arrive.start()
    for arrive, leave in ways:
        arrive.wait()
        leave.start()
    for _, leave in ways:
        leave.wait()


def place(where, query_grad, parts, after):
    counts = tuple(part.shape[0] for part in parts)
    return pl.pallas_call(
        functools.partial(place_body, counts),
        grid_spec=pltpu.PrefetchScalarGridSpec(
            num_scalar_prefetch=1,
            grid=(),
            in_specs=[pl.BlockSpec(memory_space=pl.ANY)] * (2 + len(parts)),
            out_specs=pl.BlockSpec(memory_space=pl.ANY),
            scratch_shapes=[
                pltpu.VMEM((sum(counts), TOK, QW), jnp.bfloat16),
                pltpu.SemaphoreType.DMA((sum(counts),)),
                pltpu.SemaphoreType.DMA((sum(counts),)),
            ],
        ),
        out_shape=jax.ShapeDtypeStruct(query_grad.shape, query_grad.dtype),
        input_output_aliases={1: 0},
        cost_estimate=COST,
    )(where, query_grad, after, *parts)


NT = (((1,), (1,)), ((), ()))
NN = (((1,), (0,)), ((), ()))
TN = (((0,), (0,)), ((), ()))


def dot(a, b, dims):
    return lax.dot_general(a, b, dims, preferred_element_type=jnp.float32)


def attend_body(count, base, skipped, where_ref, *refs):
    latent_ref, rope_low_ref, rope_high_ref = refs[:3]
    q_ref, d_ref, twin_q_ref, twin_d_ref = refs[3:7]
    weights = refs[7 + skipped : 7 + skipped + 2 * count]
    at = 7 + skipped + 2 * count
    sums = refs[at : at + 2] if skipped else ()
    at += len(sums)
    query_out, twin_out, latent_out, rope_out, mark_out = refs[at : at + 5]
    wk_ref, wv_ref, q_both, d_both, grad_both, dk_ref, dv_ref = refs[at + 5 :]
    step = pl.program_id(0)
    core = where_ref[0]
    key_at = lax.broadcasted_iota(jnp.int32, (SPAN, TOK), 0)
    query_at = lax.broadcasted_iota(jnp.int32, (SPAN, TOK), 1)
    inside = (key_at > query_at) & (key_at <= query_at + WIN)
    started = key_at >= jnp.where(where_ref[CHIP_AT] > 0, 0, WIN)
    masks = (inside & started, inside)

    for i in range(count):

        @pl.when(step == i)
        def _():
            wk_ref[...] = weights[2 * i][...]
            wv_ref[...] = weights[2 * i + 1][...]

    for own in range(2):

        @pl.when(core == own)
        def _():
            q_both[own] = q_ref[...]
            d_both[own] = d_ref[...]
            q_both[1 - own] = twin_q_ref[...]
            d_both[1 - own] = twin_d_ref[...]

    latent = latent_ref[...]
    keys = dot(latent, wk_ref[...], NN)
    values = dot(latent, wv_ref[...], NN).astype(jnp.bfloat16)
    low = lax.broadcasted_iota(jnp.int32, (ROWS, NOPE), 1) < ROPE
    rope_sum = jnp.zeros((ROWS, NOPE), jnp.float32)

    def fold(first, second):
        return jnp.concatenate(
            [first[:TOK], first[TOK:] + second[:WIN], second[WIN:]], axis=0
        )

    for pair in range(GROUP // 2):
        query_parts = [[], []]
        key_parts = []
        for odd in range(2):
            head = 2 * pair + odd
            key = keys[:, head * NOPE : (head + 1) * NOPE]
            if odd:
                turned = pltpu.roll(key, ROPE, 1)
                tiles = [
                    jnp.where(low, 0.0, turned).astype(jnp.bfloat16),
                    jnp.where(low, turned, rope_high_ref[...]).astype(jnp.bfloat16),
                ]
            else:
                tiles = [key.astype(jnp.bfloat16), rope_low_ref[...]]
            wide = jnp.concatenate(tiles, axis=1)
            value = values[:, head * VDIM : (head + 1) * VDIM]
            start = pair * 2 * (NOPE + ROPE) + odd * NOPE
            dk, dv = [], []
            for s in range(2):
                span = slice(s * TOK, s * TOK + SPAN)
                q = q_both[s, :, start : start + 2 * NOPE]
                d = d_both[s, :, head * VDIM : (head + 1) * VDIM]
                scores = jnp.where(masks[s], dot(wide[span], q, NT) * SCALE, -jnp.inf)
                shifted = jnp.exp(scores - jnp.max(scores, axis=0, keepdims=True))
                inverse = 1.0 / jnp.sum(shifted, axis=0, keepdims=True)
                prob_grad = dot(value[span], d, NT)
                probs = shifted * inverse
                delta = jnp.sum(probs * prob_grad, axis=0, keepdims=True)
                score_grad = (SCALE * probs * (prob_grad - delta)).astype(jnp.bfloat16)
                probs_low = probs.astype(jnp.bfloat16)
                query_parts[s].append(dot(score_grad, wide[span], TN))
                dk.append(dot(score_grad, q, NN))
                dv.append(dot(probs_low, d, NN))
            dv_ref[:, head * VDIM : (head + 1) * VDIM] = fold(*dv).astype(jnp.bfloat16)
            key_parts.append(fold(*dk))
        even, odd = key_parts
        dk_ref[:, 2 * pair * NOPE : (2 * pair + 1) * NOPE] = even[:, :NOPE].astype(jnp.bfloat16)
        dk_ref[:, (2 * pair + 1) * NOPE : (2 * pair + 2) * NOPE] = pltpu.roll(
            jnp.where(low, odd[:, NOPE:], odd[:, :NOPE]), ROPE, 1
        ).astype(jnp.bfloat16)
        rope_sum = rope_sum + jnp.where(low, even[:, NOPE:], odd[:, NOPE:])
        for s in range(2):
            first, second = query_parts[s]
            left = pair * 3 * NOPE
            grad_both[s, :, left : left + NOPE] = first[:, :NOPE].astype(jnp.bfloat16)
            grad_both[s, :, left + NOPE : left + 2 * NOPE] = (
                first[:, NOPE:] + second[:, :NOPE]
            ).astype(jnp.bfloat16)
            grad_both[s, :, left + 2 * NOPE : left + 3 * NOPE] = second[:, NOPE:].astype(
                jnp.bfloat16
            )

    latent_sum = dot(dk_ref[...], wk_ref[...], NT) + dot(dv_ref[...], wv_ref[...], NT)

    @pl.when(step == 0)
    def _():
        latent_out[...] = sums[0][...] + latent_sum if sums else latent_sum
        rope_out[...] = sums[1][...] + rope_sum if sums else rope_sum
        mark_out[...] = jnp.zeros_like(mark_out)

    @pl.when(step > 0)
    def _():
        latent_out[...] += latent_sum
        rope_out[...] += rope_sum

    for own in range(2):

        @pl.when(core == own)
        def _():
            query_out[...] = grad_both[own]
            twin_out[0] = grad_both[1 - own]


def attend(
    where, base, shared, query, out_grad, twin_query, twin_grad, weights, earlier=(), after=(), heavy=1
):
    count = len(weights)
    skipped = list(earlier[:1]) + list(after)
    head_block = lambda width: pl.BlockSpec((TOK, width), lambda g, w: (0, 2 * w[base + g] + w[0]))
    whole = lambda shape: pl.BlockSpec(shape, lambda g, w: (0,) * len(shape))
    in_specs = [
        whole((ROWS, LATENT)),
        whole((ROWS, NOPE)),
        whole((ROWS, NOPE)),
        head_block(QW),
        head_block(VW),
        head_block(QW),
        head_block(VW),
    ]
    operands = [where, *shared, query, out_grad, twin_query, twin_grad, *skipped]
    in_specs += [pl.BlockSpec(memory_space=pl.ANY)] * len(skipped)
    for (key_part, key_at), (value_part, value_at) in weights:
        in_specs.append(pl.BlockSpec((LATENT, VW), lambda g, w, at=key_at: (at, 0)))
        in_specs.append(pl.BlockSpec((LATENT, VW), lambda g, w, at=value_at: (at, 0)))
        operands += [key_part, value_part]
    if earlier:
        in_specs += [whole((ROWS, LATENT)), whole((ROWS, NOPE))]
        operands += earlier[1:]
    query_grad, part, latent_sum, rope_sum, mark = pl.pallas_call(
        functools.partial(attend_body, count, base, len(skipped)),
        grid_spec=pltpu.PrefetchScalarGridSpec(
            num_scalar_prefetch=1,
            grid=(count,),
            in_specs=in_specs,
            out_specs=[
                head_block(QW),
                pl.BlockSpec((1, TOK, QW), lambda g, w: (g, 0, 0)),
                whole((ROWS, LATENT)),
                whole((ROWS, NOPE)),
                whole((8, NOPE)),
            ],
            scratch_shapes=[
                pltpu.VMEM((LATENT, VW), jnp.bfloat16),
                pltpu.VMEM((LATENT, VW), jnp.bfloat16),
                pltpu.VMEM((2, TOK, QW), jnp.bfloat16),
                pltpu.VMEM((2, TOK, VW), jnp.bfloat16),
                pltpu.VMEM((2, TOK, QW), jnp.bfloat16),
                pltpu.VMEM((ROWS, VW), jnp.bfloat16),
                pltpu.VMEM((ROWS, VW), jnp.bfloat16),
            ],
        ),
        out_shape=[
            jax.ShapeDtypeStruct((TOK, HEADS * (NOPE + ROPE)), jnp.bfloat16),
            jax.ShapeDtypeStruct((count, TOK, QW), jnp.bfloat16),
            jax.ShapeDtypeStruct((ROWS, LATENT), jnp.float32),
            jax.ShapeDtypeStruct((ROWS, NOPE), jnp.float32),
            jax.ShapeDtypeStruct((8, NOPE), jnp.float32),
        ],
        input_output_aliases={8: 0} if earlier else {},
        compiler_params=pltpu.CompilerParams(vmem_limit_bytes=60 * 1024 * 1024),
        cost_estimate=pl.CostEstimate(
            flops=heavy * count * 500_000_000, bytes_accessed=count * 500_000, transcendentals=0
        ),
    )(*operands)
    return query_grad, latent_sum, rope_sum, part, mark


def terms_body(where_ref, rows_ref, own_ref, other_ref, *refs):
    out_ref = refs[-1]
    here = where_ref[HALF_AT] * (EXP * CAP)
    there = (1 - where_ref[HALF_AT]) * (EXP * CAP)

    def rows(at):
        part = rows_ref[:, 0, pl.ds(pl.multiple_of(at, EXP * CAP), EXP * CAP), :]
        return part.reshape(4 * EXP * CAP, -1)

    total = dot(rows(here), own_ref[...], NN) + dot(rows(there), other_ref[...], NN)
    out_ref[...] = total.astype(jnp.bfloat16).reshape(out_ref.shape)


def terms(where, twin, slices, own_down, other_down, after):
    rows = slices.reshape(4, 2, 2 * EXP * CAP, -1)
    depth = rows.shape[3]
    weight = pl.BlockSpec((depth, FFH), lambda g, w: (0, 0))
    number = (lambda w: 1 - w[0]) if twin else (lambda w: w[0])
    return pl.pallas_call(
        terms_body,
        grid_spec=pltpu.PrefetchScalarGridSpec(
            num_scalar_prefetch=1,
            grid=(1,),
            in_specs=[
                pl.BlockSpec(
                    (4, 1, 2 * EXP * CAP, depth), lambda g, w: (0, number(w), 0, 0)
                ),
                weight,
                weight,
            ]
            + [pl.BlockSpec(memory_space=pl.ANY)] * len(after),
            out_specs=pl.BlockSpec((4, EXP * CAP, FFH), lambda g, w: (0, 0, 0)),
        ),
        out_shape=jax.ShapeDtypeStruct((4, EXP * CAP, FFH), jnp.bfloat16),
        compiler_params=pltpu.CompilerParams(vmem_limit_bytes=60 * 1024 * 1024),
        cost_estimate=pl.CostEstimate(
            flops=100_000_000, bytes_accessed=100_000, transcendentals=0
        ),
    )(where, rows, own_down, other_down, *after)


def local(
    query,
    out_grad,
    latent,
    rope_key,
    w_key,
    w_value,
    grad_stream,
    expert_ids,
    gate_weights,
    saved_hidden,
    w_down,
):
    query, out_grad, latent, rope_key = query[0], out_grad[0], latent[0], rope_key[0]
    grad_stream, expert_ids, gate_weights = grad_stream[0], expert_ids[0], gate_weights[0]
    index = lax.axis_index("ctx")
    core = index % 2
    chip = index // 2
    x = chip // 2
    half = chip % 2

    def group(step, flip):
        return 2 * ((x + step) % 4) + (half ^ flip)

    groups = [
        group(0, 0),
        group(-1, 0),
        group(1, 0),
        group(0, 1),
        group(2, 0),
        group(-1, 1),
        group(1, 1),
        group(2, 1),
    ]
    where = jnp.stack([core, *groups, chip, half]).astype(jnp.int32)

    def both(stack):
        return ((stack, 0), (stack, 1))

    mine = join(latent, rope_key.T)
    twin_rows = lax.ppermute(mine, "ctx", TWIN)
    halo = lax.ppermute(
        jnp.where(core == 0, twin_rows[TOK - WIN :], mine[TOK - WIN :]), "ctx", [(i, i + 2) for i in range(CTX - 2)]
    )
    own = stack(w_key, w_value)
    before = lax.ppermute(own, "ctx", RIGHT)
    after = lax.ppermute(own, "ctx", LEFT)
    beside = lax.ppermute(own, ("ctx", "exp"), ACROSS)
    twin_query = lax.ppermute(query, "ctx", TWIN)
    twin_grad = lax.ppermute(out_grad, "ctx", TWIN)
    down = w_down[0].T
    other_down = lax.ppermute(down, "ctx", [(i, i ^ 2) for i in range(CTX)])

    share = EXPERTS // EXP
    slots = jnp.arange(EXP * CAP, dtype=jnp.int32)[None, :]
    ids = tie(expert_ids, own)
    match = [ids[:, k : k + 1] == slots // CAP * share for k in range(TOPK)]
    live = functools.reduce(jnp.logical_or, match)
    token_at = jnp.arange(TOK, dtype=jnp.int32)
    earlier = dot(
        (token_at[:, None] > token_at[None, :]).astype(jnp.bfloat16), live.astype(jnp.bfloat16), NN
    )
    token_hot = (live & (earlier == (slots % CAP).astype(jnp.float32))).astype(jnp.bfloat16)
    gates = sum(
        jnp.where(match[k], gate_weights[:, k : k + 1].astype(jnp.float32), 0.0)
        for k in range(TOPK)
    )
    gate_send = jnp.sum(token_hot.astype(jnp.float32) * gates, axis=0).reshape(EXP, 1, CAP)
    outbound = dot(token_hot, grad_stream, TN).astype(jnp.bfloat16)
    tiles = outbound.shape[1] // NOPE
    outbound = jnp.concatenate(
        [
            outbound.reshape(EXP, CAP * tiles, NOPE),
            jnp.pad(gate_send.astype(jnp.bfloat16), ((0, 0), (0, 7), (0, NOPE - CAP))),
        ],
        axis=1,
    )
    outbound = tie(outbound, twin_query, own)
    routed = lax.all_to_all(outbound, "exp", split_axis=0, concat_axis=0, tiled=True)

    shared = prepare(where, mine, twin_rows, halo)
    common = (shared, query, out_grad, twin_query, twin_grad)

    opposite = lax.ppermute(before, "ctx", RIGHT)
    beside_after = lax.ppermute(beside, "ctx", LEFT)
    beside_before = lax.ppermute(before, ("ctx", "exp"), ACROSS)
    *sums, part_b, mark_b = attend(
        where, 1, *common, [both(own), both(before), both(after)], heavy=10
    )
    routed = tie(routed, mark_b, other_down)
    row_gate = routed[:, CAP * tiles, :CAP].reshape(EXP * CAP, 1)
    slices = routed[:, : CAP * tiles].reshape(EXP * CAP, 4, 2, 2, -1)
    slices = slices.transpose(1, 3, 2, 0, 4).reshape(CHIPS, 2 * EXP * CAP, -1)
    sent = slices
    slices = lax.all_to_all(
        slices, "ctx", split_axis=0, concat_axis=0, tiled=True, axis_index_groups=RING
    )

    *sums, part_d, mark_d = attend(
        where, 4, *common, [both(beside), both(opposite)], sums, (sent,)
    )
    part_d = lax.ppermute(part_d, "ctx", TWIN)
    part_b = lax.ppermute(part_b, "ctx", TWIN)

    beside_after = tie(beside_after, mark_d)
    key_half = beside_after[:LATENT]
    value_half = tie(opposite[LATENT:], mark_d)
    last_key = lax.ppermute(key_half, "ctx", LEFT)
    last_value = lax.ppermute(value_half, ("ctx", "exp"), ACROSS)

    give = terms(
        where, True, slices, down, other_down, (mark_b, beside_before, key_half, value_half)
    )
    keep = terms(where, False, slices, down, other_down, (give,))
    taken = lax.ppermute(give, "ctx", TWIN)

    keep = (keep.astype(jnp.float32) + taken.astype(jnp.float32)).astype(jnp.bfloat16)
    pieces = lax.all_to_all(
        keep, "ctx", split_axis=0, concat_axis=0, tiled=True, axis_index_groups=RING_CORE
    )

    *sums, part_c, mark_c = attend(
        where,
        6,
        *common,
        [
            both(beside_before),
            both(beside_after),
            ((last_key, 0), (last_value, 0)),
        ],
        sums,
        (keep,),
    )
    part_c = lax.ppermute(part_c, "ctx", TWIN)

    query_grad, latent_sum, rope_sum = sums
    latent_sum = tie(latent_sum, pieces)
    sums = jnp.concatenate([latent_sum, rope_sum[:, :ROPE] + rope_sum[:, ROPE:]], axis=1)
    back = lax.ppermute(sums[:WIN], "ctx", [(i + 2, i) for i in range(CTX - 2)])
    low = sums[WIN : WIN + TOK]
    high = sums[WIN + TOK :]
    high = jnp.concatenate([high[: TOK - WIN], high[TOK - WIN :] + back], axis=0)
    kept = jnp.where(core == 0, low, high)
    given = lax.ppermute(jnp.where(core == 0, high, low), "ctx", TWIN)
    total = (kept + given).astype(jnp.bfloat16)
    raw_grad = jnp.sum(pieces.astype(jnp.float32), axis=0)
    gate_part = jnp.sum(saved_hidden[0, 0].astype(jnp.float32) * raw_grad, axis=1)
    hidden_grad = (row_gate.astype(jnp.float32) * raw_grad).astype(jnp.bfloat16)
    returned = lax.all_to_all(
        gate_part.reshape(EXP, CAP), "exp", split_axis=0, concat_axis=0, tiled=True
    )
    query_grad = place(where, query_grad, (part_b, part_d, part_c), gate_part[None])
    found = token_hot.astype(jnp.float32) * returned.reshape(1, -1)
    gate_grad = jnp.stack(
        [jnp.sum(jnp.where(match[k], found, 0.0), axis=1) for k in range(TOPK)], axis=1
    )
    return (
        query_grad[None],
        total[None, :, :LATENT],
        total[None, :, LATENT:],
        hidden_grad[None, None],
        gate_grad[None],
    )


def solution(mesh):
    in_specs = (
        P("exp", "ctx", None),
        P("exp", "ctx", None),
        P("exp", "ctx", None),
        P("exp", "ctx", None),
        P(None, "ctx"),
        P(None, "ctx"),
        P("exp", "ctx", None),
        P("exp", "ctx", None),
        P("exp", "ctx", None),
        P("ctx", "exp", None, None),
        P("exp", None, "ctx"),
    )
    out_specs = (
        P("exp", "ctx", None),
        P("exp", "ctx", None),
        P("exp", "ctx", None),
        P("ctx", "exp", None, None),
        P("exp", "ctx", None),
    )
    return jax.shard_map(local, mesh=mesh, in_specs=in_specs, out_specs=out_specs, check_vma=False)
```
